32 devices in a mesh: gx: 8 (over z, x), gy: 4 (over y, core).
Axes of the slice: x: 2, y: 2, z: 4, core: 2. Of those that a mesh axis runs over, the one named last changes fastest.
Arguments:
- tokens: bfloat16 [128, 64, 2, 512], P('gx', 'gy'), may hold values from -6 to 6
- cotangent: bfloat16 [128, 64, 2, 512], P('gx', 'gy'), may hold values from -6 to 6
- gain_x: float32 [512], replicated, may hold values from 0.1 to 1.9
- w_qkv_x: bfloat16 [512, 1536], replicated, may hold values from -5 to 5, as said below
- w_out_x: bfloat16 [512, 512], replicated, may hold values from -0.25 to 0.25
- gain_y: float32 [512], replicated, may hold values from 0.1 to 1.9
- w_qkv_y: bfloat16 [512, 1536], replicated, may hold values from -5 to 5, as said below
- w_out_y: bfloat16 [512, 512], replicated, may hold values from -0.25 to 0.25
- gain_mlp: float32 [512], replicated, may hold values from 0.1 to 1.9
- w_up: bfloat16 [512, 2048], replicated, may hold values from -0.25 to 0.25
- w_down: bfloat16 [2048, 512], replicated, may hold values from -0.125 to 0.125
Outputs:
- grad_tokens: bfloat16 [128, 64, 2, 512], P('gx', 'gy')
The draws below stay inside these ranges and needn't reach their ends.
Inputs may be any that keep to these rules, and one draw needn't show every extreme that they name: `w_qkv_x`: query, key and value projections side by side. `w_qkv_y`: query, key and value projections side by side.
All inputs are finite; a program needn't handle non-finite values.
Results may differ from the reference program's by a relative error of at most 0.013.
Values may be sent and summed in bfloat16 or wider, within the bound.
No kernel may reach another device: no remote copies, remote signals or barrier semaphores. Data moves between devices by JAX's collectives and lax.ppermute only.
A program may use at most 128 MiB of HBM per device.

```python
from functools import partial
import jax
import jax.numpy as jnp
from jax import lax

D = 512
HEADS = 8
FF = 2048
DEPTH = 2
LX = 128
LY = 64


def qkv_weights(key, salt):
    base = jax.random.fold_in(key, salt)
    first = jax.random.fold_in(base, 0)
    second = jax.random.fold_in(base, 1)
    fourth = jax.random.fold_in(base, 3)
    scale = D ** (-0.5)
    query_cols = jnp.clip(jax.random.normal(first, (D, D), jnp.float32), -4.0, 4.0) * scale
    key_cols = jnp.clip(jax.random.normal(second, (D, D), jnp.float32), -4.0, 4.0) * scale
    value_cols = jnp.clip(jax.random.normal(fourth, (D, D), jnp.float32), -4.0, 4.0) * scale
    return jnp.concatenate([query_cols, key_cols, value_cols], 1).astype(jnp.bfloat16)


def draw_w_qkv_x(key, part):
    return qkv_weights(key, 11)


def draw_w_qkv_y(key, part):
    return qkv_weights(key, 12)


def block_levels(own_key, shape, pieces, least, top_value):
    def one(dim, parts):
        draws = jax.random.uniform(jax.random.fold_in(jax.random.fold_in(own_key, 6), dim), (parts,), jnp.float32, least / len(pieces), top_value / len(pieces))
        return jnp.repeat(jnp.exp(draws), shape[dim] // parts).reshape((-1,) + (1,) * (len(shape) - dim - 1))

    factor_of = one(*pieces[0])
    for cut in pieces[1:]:
        factor_of = factor_of * one(*cut)
    return factor_of


def normal_values(rng, extent, width, limit, cuts=(), held_as=jnp.bfloat16):
    values = width * jax.random.normal(rng, extent, jnp.float32)
    if cuts:
        values = values * block_levels(rng, extent, cuts, -0.22, 0.18)
    return jnp.clip(values, -limit, limit).astype(held_as)


def setup_inputs(seed: int = 0) -> dict:
    keys = jax.random.split(jax.random.key(seed), 12)
    tokens = normal_values(keys[0], (LX, LY, DEPTH, D), 1.0, 6.0, ((0, 8), (1, 4)))
    cotangent = normal_values(keys[1], (LX, LY, DEPTH, D), 1.0, 6.0, ((0, 8), (1, 4)))
    gain_x = jnp.clip(1.0 + 0.18 * jax.random.normal(keys[2], (D,), jnp.float32), 0.1, 1.9)
    w_qkv_x = draw_w_qkv_x(jax.random.fold_in(keys[11], 71), 0)
    w_out_x = normal_values(keys[4], (D, D), D ** -0.5, 0.25)
    gain_y = jnp.clip(1.0 + 0.18 * jax.random.normal(keys[5], (D,), jnp.float32), 0.1, 1.9)
    w_qkv_y = draw_w_qkv_y(jax.random.fold_in(keys[11], 71), 0)
    w_out_y = normal_values(keys[7], (D, D), D ** -0.5, 0.25)
    gain_mlp = jnp.clip(1.0 + 0.18 * jax.random.normal(keys[8], (D,), jnp.float32), 0.1, 1.9)
    w_up = normal_values(keys[9], (D, FF), D ** -0.5, 0.25)
    w_down = normal_values(keys[10], (FF, D), FF ** -0.5, 0.125)
    return dict(tokens=tokens, cotangent=cotangent, gain_x=gain_x, w_qkv_x=w_qkv_x, w_out_x=w_out_x, gain_y=gain_y, w_qkv_y=w_qkv_y, w_out_y=w_out_y, gain_mlp=gain_mlp, w_up=w_up, w_down=w_down)


def to_low(tensor):
    return lax.optimization_barrier(tensor.astype(jnp.bfloat16))

def layer_norm(inputs, norm_gain):
    average = lax.optimization_barrier(jnp.mean(inputs, -1, keepdims=True))
    centred = inputs - average
    variance = lax.optimization_barrier(jnp.mean(centred * centred, -1, keepdims=True))
    return centred * lax.rsqrt(variance + 1e-05) * norm_gain

def norm_back(inputs, norm_gain, gradient):
    _, pullback = jax.vjp(lambda tensor: layer_norm(tensor, norm_gain), inputs)
    return pullback(gradient)[0]

def project(tensor, weight):
    lead_dims = tensor.shape[:-1]
    flattened = tensor.reshape(-1, tensor.shape[-1])
    result = jnp.dot(flattened, weight, preferred_element_type=jnp.float32)
    return result.reshape(lead_dims + (weight.shape[1],))

def project_back(tensor, weight):
    lead_dims = tensor.shape[:-1]
    flattened = tensor.reshape(-1, tensor.shape[-1])
    result = lax.dot_general(flattened, weight, (((1,), (1,)), ((), ())), preferred_element_type=jnp.float32)
    return result.reshape(lead_dims + (weight.shape[0],))

def heads_of(tensor, which_part):
    lead_dims = tensor.shape[:-1]
    block_part = tensor[..., which_part * D:(which_part + 1) * D]
    return block_part.astype(jnp.float32).reshape(lead_dims + (HEADS, D // HEADS))

def softmax_rows(queries, key_part):
    scores = jnp.einsum('qzhd,kzhd->zhqk', queries, key_part) * (D // HEADS) ** (-0.5)
    highest = lax.optimization_barrier(jnp.max(scores, -1, keepdims=True))
    exponent = jnp.exp(scores - highest)
    return exponent / lax.optimization_barrier(jnp.sum(exponent, -1, keepdims=True))

def attend_slab(qkv_proj):
    queries, key_part, value_part = (heads_of(qkv_proj, 0), heads_of(qkv_proj, 1), heads_of(qkv_proj, 2))
    probs = softmax_rows(queries, key_part)
    probs_low = to_low(probs).astype(jnp.float32)
    result = jnp.einsum('zhqk,kzhd->qzhd', probs_low, value_part)
    return to_low(result.reshape(qkv_proj.shape[:-1] + (D,)))

def back_slab(qkv_proj, grad_out):
    queries, key_part, value_part = (heads_of(qkv_proj, 0), heads_of(qkv_proj, 1), heads_of(qkv_proj, 2))
    scale = (D // HEADS) ** (-0.5)
    probs = softmax_rows(queries, key_part)
    probs_low = to_low(probs).astype(jnp.float32)
    grad_heads = heads_of(grad_out, 0)
    grad_probs = jnp.einsum('qzhd,kzhd->zhqk', grad_heads, value_part)
    grad_scores = probs * (grad_probs - lax.optimization_barrier(jnp.sum(probs * grad_probs, -1, keepdims=True)))
    grad_low = to_low(grad_scores).astype(jnp.float32)
    grad_q = to_low(jnp.einsum('zhqk,kzhd->qzhd', grad_low, key_part) * scale)
    grad_k = to_low(jnp.einsum('zhqk,qzhd->kzhd', grad_low, queries) * scale)
    grad_v = to_low(jnp.einsum('zhqk,qzhd->kzhd', probs_low, grad_heads))
    lead_dims = qkv_proj.shape[:-1] + (D,)
    return jnp.concatenate([grad_q.reshape(lead_dims), grad_k.reshape(lead_dims), grad_v.reshape(lead_dims)], -1)

def along_x(action, *arrays):
    moved = tuple((jnp.moveaxis(member, 1, 0) for member in arrays))
    result = lax.map(lambda slabs: action(*slabs), moved)
    return jnp.moveaxis(result, 0, 1)

def along_y(action, *arrays):
    return lax.map(lambda slabs: action(*slabs), tuple(arrays))

def reference(tokens, cotangent, gain_x, w_qkv_x, w_out_x, gain_y, w_qkv_y, w_out_y, gain_mlp, w_up, w_down):
    stream_0 = tokens.astype(jnp.float32)
    qkv_x = to_low(project(to_low(layer_norm(stream_0, gain_x)), w_qkv_x))
    mixed_x = along_x(attend_slab, qkv_x)
    stream_1 = to_low(stream_0 + project(mixed_x, w_out_x))
    stream_1f = stream_1.astype(jnp.float32)
    qkv_y = to_low(project(to_low(layer_norm(stream_1f, gain_y)), w_qkv_y))
    mixed_y = along_y(attend_slab, qkv_y)
    stream_2 = to_low(stream_1f + project(mixed_y, w_out_y))
    stream_2f = stream_2.astype(jnp.float32)
    pre_act = project(to_low(layer_norm(stream_2f, gain_mlp)), w_up)
    grad_act = to_low(project_back(cotangent, w_down))
    _, pullback = jax.vjp(partial(jax.nn.gelu, approximate=True), pre_act)
    grad_pre = to_low(pullback(grad_act.astype(jnp.float32))[0])
    grad_2 = to_low(cotangent.astype(jnp.float32) + norm_back(stream_2f, gain_mlp, project_back(grad_pre, w_up)))
    grad_mixed_y = to_low(project_back(grad_2, w_out_y))
    grad_qkv_y = along_y(back_slab, qkv_y, grad_mixed_y)
    grad_1 = to_low(grad_2.astype(jnp.float32) + norm_back(stream_1f, gain_y, project_back(grad_qkv_y, w_qkv_y)))
    grad_mixed_x = to_low(project_back(grad_1, w_out_x))
    grad_qkv_x = along_x(back_slab, qkv_x, grad_mixed_x)
    grad_tokens = to_low(grad_1.astype(jnp.float32) + norm_back(stream_0, gain_x, project_back(grad_qkv_x, w_qkv_x)))
    return grad_tokens
```

```python
import jax
import jax.numpy as jnp
import numpy as np
from jax import lax
from jax.experimental import pallas as pl
from jax.experimental.pallas import tpu as pltpu
from jax.sharding import Mesh
from jax.sharding import PartitionSpec as P

HEADS = 8
NZ = 2
EPS = 1e-05
F32 = jnp.float32
BF16 = jnp.bfloat16
VMEM_LIMIT = 56 * 1024 * 1024


def dot(a, b):
    return jnp.dot(a, b, preferred_element_type=F32)


def dot_t(a, b):
    return lax.dot_general(a, b, (((1,), (1,)), ((), ())), preferred_element_type=F32)


def dot_lt(a, b):
    return lax.dot_general(a, b, (((0,), (0,)), ((), ())), preferred_element_type=F32)


def one_hot(target):
    size = target.shape[1]
    rows = lax.broadcasted_iota(jnp.int32, (size, size), 0)
    return jnp.where(rows == target, 1.0, 0.0).astype(BF16)


def standardize(x):
    centred = x - jnp.mean(x, -1, keepdims=True)
    inv = lax.rsqrt(jnp.mean(centred * centred, -1, keepdims=True) + EPS)
    return centred * inv, inv


def norm_back(x, gain, grad):
    unit, inv = standardize(x)
    scaled = grad * gain
    return inv * (
        scaled
        - jnp.mean(scaled, -1, keepdims=True)
        - unit * jnp.mean(scaled * unit, -1, keepdims=True)
    )


def group_of(length, dim):
    return 4 if length * 4 <= 256 and HEADS % 4 == 0 else 2


def spread(block, count):
    width = block.shape[1] // count
    lane = lax.broadcasted_iota(jnp.int32, block.shape, 1)
    zero = jnp.zeros_like(block)
    return jnp.concatenate(
        [
            jnp.where((lane >= i * width) & (lane < (i + 1) * width), block, zero)
            for i in range(count)
        ],
        0,
    )


def gather(block, count):
    rows = block.shape[0] // count
    width = block.shape[1] // count
    lane = lax.broadcasted_iota(jnp.int32, (rows, block.shape[1]), 1)
    result = block[:rows]
    for i in range(1, count):
        result = jnp.where(lane >= i * width, block[i * rows : (i + 1) * rows], result)
    return result


def probs_t(q_wide, k):
    scores = dot_t(k, q_wide)
    exponent = jnp.exp(scores - jnp.max(scores, 0, keepdims=True))
    return exponent * (1.0 / jnp.sum(exponent, 0, keepdims=True))


def attend_line(qkv, rows, dim, length, mixed, keep=None):
    count = group_of(length, dim)
    width = dim // HEADS * count
    scale = (dim // HEADS) ** -0.5
    for j in range(HEADS // count):
        q = qkv[rows, j * width : (j + 1) * width] * jnp.array(scale, BF16)
        k = qkv[rows, dim + j * width : dim + (j + 1) * width]
        v = qkv[rows, 2 * dim + j * width : 2 * dim + (j + 1) * width]
        probs = probs_t(spread(q, count), k)
        if keep is not None:
            keep(j, probs)
        out = dot_lt(probs.astype(BF16), v)
        mixed[rows, j * width : (j + 1) * width] = gather(out, count).astype(BF16)


def attend_back_line(qkv, rows, dim, length, grad, grad_qkv, kept=None):
    count = group_of(length, dim)
    width = dim // HEADS * count
    scale = (dim // HEADS) ** -0.5
    for j in range(HEADS // count):
        lanes = slice(j * width, (j + 1) * width)
        q = qkv[rows, lanes] * jnp.array(scale, BF16)
        k = qkv[rows, dim + j * width : dim + (j + 1) * width]
        v = qkv[rows, 2 * dim + j * width : 2 * dim + (j + 1) * width]
        q_wide = spread(q, count)
        g_wide = spread(grad[rows, lanes], count)
        probs = probs_t(q_wide, k) if kept is None else kept(j)
        g_probs = dot_t(v, g_wide)
        weighted = probs * g_probs
        g_scores = (weighted - probs * jnp.sum(weighted, 0, keepdims=True)).astype(BF16)
        g_q = gather(dot_lt(g_scores, k), count) * scale
        g_k = dot(g_scores, q_wide)
        g_v = dot(probs.astype(BF16), g_wide)
        grad_qkv[rows, lanes] = g_q.astype(BF16)
        grad_qkv[rows, dim + j * width : dim + (j + 1) * width] = g_k.astype(BF16)
        grad_qkv[rows, 2 * dim + j * width : 2 * dim + (j + 1) * width] = g_v.astype(BF16)


def line_rows(i, length):
    return pl.ds(pl.multiple_of(i * length, length), length)


def reorder_body(target, src, out):
    out[...] = dot(one_hot(target[...]), src[...]).astype(BF16)


def reorder(target, src):
    return pl.pallas_call(
        reorder_body,
        out_shape=jax.ShapeDtypeStruct(src.shape, BF16),
        compiler_params=pltpu.CompilerParams(vmem_limit_bytes=VMEM_LIMIT),
        name="reorder",
    )(target, src)


def x_forward_body(target, tok, gain, w_qkv, w_out, sent, qkv, normed, mixed):
    blocks, lines, part, dim = tok.shape
    length = blocks * part

    def norm_line(i, _):
        x = tok[:, i].reshape(length, dim).astype(F32)
        unit, _ = standardize(x)
        normed[line_rows(i, length), :] = (unit * gain[...]).astype(BF16)
        return 0

    lax.fori_loop(0, lines, norm_line, 0)
    for j in range(3):
        cols = slice(j * dim, (j + 1) * dim)
        qkv[:, cols] = dot(normed[...], w_qkv[:, cols]).astype(BF16)

    def attend(i, _):
        attend_line(qkv, line_rows(i, length), dim, length, mixed)
        return 0

    lax.fori_loop(0, lines, attend, 0)

    def project(i, _):
        rows = line_rows(i, length)
        x = tok[:, i].reshape(length, dim).astype(F32)
        normed[rows, :] = (x + dot(mixed[rows, :], w_out[...])).astype(BF16)
        return 0

    lax.fori_loop(0, lines, project, 0)
    sent[...] = dot(one_hot(target[...]), normed[...]).astype(BF16)


def middle_body(
    to_line, to_sent, s1_in, cot_in, gain_y, w_qkv, w_out, gain_m, w_up, w_down, sent,
    s1, cot, normed, qkv, mixed, s2, probs_kept, acc, grad, grad_qkv,
):
    blocks, lines, part, dim = cot_in.shape
    length = blocks * part
    hidden = w_up.shape[1]
    s1[...] = dot(one_hot(to_line[...]), s1_in[...]).astype(BF16)

    def norm_line(i, _):
        rows = line_rows(i, length)
        cot[rows, :] = cot_in[:, i].reshape(length, dim)
        unit, _ = standardize(s1[rows, :].astype(F32))
        normed[rows, :] = (unit * gain_y[...]).astype(BF16)
        return 0

    lax.fori_loop(0, lines, norm_line, 0)
    for j in range(3):
        cols = slice(j * dim, (j + 1) * dim)
        qkv[:, cols] = dot(normed[...], w_qkv[:, cols]).astype(BF16)

    def attend(i, _):
        def keep(j, probs):
            probs_kept[i, j] = probs

        attend_line(qkv, line_rows(i, length), dim, length, mixed, keep)
        return 0

    lax.fori_loop(0, lines, attend, 0)
    tile = 128
    tiles = s1.shape[0] // tile

    def project(i, _):
        rows = line_rows(i, tile)
        low = (s1[rows, :].astype(F32) + dot(mixed[rows, :], w_out[...])).astype(BF16)
        s2[rows, :] = low
        unit, _ = standardize(low.astype(F32))
        normed[rows, :] = (unit * gain_m[...]).astype(BF16)
        return 0

    lax.fori_loop(0, tiles, project, 0)

    chunk = 512 if hidden % 512 == 0 else hidden
    c0 = 0.7978845608028654
    c1 = 0.044715
    for c in range(hidden // chunk):
        cols = slice(c * chunk, (c + 1) * chunk)

        def mlp(i, _):
            rows = line_rows(i, tile)
            pre = dot(normed[rows, :], w_up[:, cols])
            g_act = dot_t(cot[rows, :], w_down[cols, :]).astype(BF16).astype(F32)
            square = pre * pre
            half = 0.5 * jnp.tanh(pre * (c0 + (c0 * c1) * square)) + 0.5
            slope = half + pre * (half - half * half) * (2 * c0 + (6 * c0 * c1) * square)
            g_pre = (g_act * slope).astype(BF16)
            part_sum = dot_t(g_pre, w_up[:, cols])
            acc[rows, :] = part_sum if c == 0 else acc[rows, :] + part_sum
            return 0

        lax.fori_loop(0, tiles, mlp, 0)

    def back_norm_mlp(i, _):
        rows = line_rows(i, tile)
        g2 = cot[rows, :].astype(F32) + norm_back(
            s2[rows, :].astype(F32), gain_m[...], acc[rows, :]
        )
        cot[rows, :] = g2.astype(BF16)
        grad[rows, :] = dot_t(cot[rows, :], w_out[...]).astype(BF16)
        return 0

    lax.fori_loop(0, tiles, back_norm_mlp, 0)

    def attend_back(i, _):
        attend_back_line(
            qkv, line_rows(i, length), dim, length, grad, grad_qkv, lambda j: probs_kept[i, j]
        )
        return 0

    lax.fori_loop(0, lines, attend_back, 0)

    def back_norm(i, _):
        rows = line_rows(i, tile)
        g_normed = dot_t(grad_qkv[rows, :], w_qkv[...])
        g1 = cot[rows, :].astype(F32) + norm_back(
            s1[rows, :].astype(F32), gain_y[...], g_normed
        )
        normed[rows, :] = g1.astype(BF16)
        return 0

    lax.fori_loop(0, tiles, back_norm, 0)
    sent[...] = dot(one_hot(to_sent[...]), normed[...]).astype(BF16)


def x_back_body(to_line, g1_in, tok, qkv, gain, w_qkv, w_out, sent, g1, grad, grad_qkv):
    blocks, lines, part, dim = tok.shape
    length = blocks * part
    g1[...] = dot(one_hot(to_line[...]), g1_in[...]).astype(BF16)
    grad[...] = dot_t(g1[...], w_out[...]).astype(BF16)

    def attend_back(i, _):
        attend_back_line(qkv, line_rows(i, length), dim, length, grad, grad_qkv)
        return 0

    lax.fori_loop(0, lines, attend_back, 0)

    def back_norm(i, _):
        rows = line_rows(i, length)
        x = tok[:, i].reshape(length, dim).astype(F32)
        g_normed = dot_t(grad_qkv[rows, :], w_qkv[...])
        total = g1[rows, :].astype(F32) + norm_back(x, gain[...], g_normed)
        sent[:, i] = total.astype(BF16).reshape(blocks, part, dim)
        return 0

    lax.fori_loop(0, lines, back_norm, 0)


def call(body, outs, scratch, name, flops, *args):
    return pl.pallas_call(
        body,
        out_shape=outs,
        scratch_shapes=scratch,
        compiler_params=pltpu.CompilerParams(vmem_limit_bytes=VMEM_LIMIT),
        cost_estimate=pl.CostEstimate(flops=flops, bytes_accessed=4000000, transcendentals=0),
        name=name,
    )(*args)


def inverse(order):
    result = np.empty_like(order)
    result[order] = np.arange(order.size, dtype=order.dtype)
    return result


def row(order):
    return np.asarray(order, np.int32).reshape(1, -1)


def make_local(halves, gh, gy):
    gx = halves * gh

    def local(
        tokens, cotangent, gain_x, w_qkv_x, w_out_x, gain_y, w_qkv_y, w_out_y, gain_mlp, w_up,
        w_down,
    ):
        tx, ty, tz, dim = tokens.shape
        count = tx * ty * tz
        y_lines = ty // gh
        x_lines = tz * tx // gy
        len_x, len_y = tx * gx, ty * gy
        mine = lax.axis_index("gz")

        tile_row = np.arange(count).reshape(tx, ty, tz)
        tok_order = tile_row.reshape(tx, gh, y_lines, tz).transpose(3, 1, 2, 0).reshape(-1)
        cot_orders = [
            tile_row.transpose(2, 0, 1)[[z, 1 - z]].reshape(-1) for z in range(halves)
        ]
        line_row = np.arange(count).reshape(y_lines, halves, gh, tx)
        out_orders = []
        for z in range(halves):
            own_first = line_row[:, [z, 1 - z]]
            cut = own_first.transpose(0, 2, 1, 3).reshape(y_lines, gh, gy, x_lines)
            out_orders.append(cut.transpose(2, 1, 0, 3).reshape(-1))
        y_order = np.arange(count).reshape(gy * gh * y_lines, x_lines).T.reshape(-1)

        def pick(options):
            return jnp.where(mine == 0, row(options[0]), row(options[1]))

        def vm(shape, dtype=BF16):
            return pltpu.VMEM(shape, dtype)

        flat = jax.ShapeDtypeStruct((count, dim), BF16)
        gain_x, gain_y, gain_mlp = (g.reshape(1, dim) for g in (gain_x, gain_y, gain_mlp))

        tok_sent = reorder(row(inverse(tok_order)), tokens.reshape(count, dim))
        tok_x = lax.all_to_all(
            tok_sent.reshape(gx, count // gx, dim), ("gz", "gh"), 0, 0, tiled=True
        ).reshape(gx, y_lines, tx, dim)

        cot_sent = reorder(pick([inverse(o) for o in cot_orders]), cotangent.reshape(count, dim))
        other = lax.ppermute(cot_sent[count // 2 :], "gz", [(0, 1), (1, 0)])
        cot_pair = jnp.concatenate([cot_sent[: count // 2], other], 0)
        cot_y = lax.all_to_all(
            cot_pair.reshape(gy, count // gy, dim), "gy", 0, 0, tiled=True
        ).reshape(gy, x_lines, ty, dim)

        sent, qkv_x = call(
            x_forward_body,
            (flat, jax.ShapeDtypeStruct((count, 3 * dim), BF16)),
            [vm((count, dim)), vm((count, dim))],
            "x_forward",
            3 * 10**9,
            pick([inverse(o) for o in out_orders]),
            tok_x, gain_x, w_qkv_x, w_out_x,
        )
        s1_y = lax.all_to_all(
            sent.reshape(gh * gy, count // (gh * gy), dim), ("gy", "gh"), 0, 0, tiled=True
        ).reshape(count, dim)

        group = group_of(len_y, dim)
        g1_sent = call(
            middle_body,
            flat,
            [
                vm((count, dim)),
                vm((count, dim)),
                vm((count, dim)),
                vm((count, 3 * dim)),
                vm((count, dim)),
                vm((count, dim)),
                vm((x_lines, HEADS // group, len_y, group * len_y), F32),
                vm((count, dim), F32),
                vm((count, dim)),
                vm((count, 3 * dim)),
            ],
            "middle",
            9 * 10**9,
            row(inverse(y_order)), row(y_order),
            s1_y, cot_y, gain_y, w_qkv_y, w_out_y, gain_mlp, w_up, w_down,
        )
        g1_x = lax.all_to_all(
            g1_sent.reshape(gh * gy, count // (gh * gy), dim), ("gy", "gh"), 0, 0, tiled=True
        ).reshape(count, dim)

        gt_sent = call(
            x_back_body,
            jax.ShapeDtypeStruct(tok_x.shape, BF16),
            [vm((count, dim)), vm((count, dim)), vm((count, 3 * dim))],
            "x_back",
            3 * 10**9,
            pick(out_orders),
            g1_x, tok_x, qkv_x, gain_x, w_qkv_x, w_out_x,
        )
        gt = lax.all_to_all(
            gt_sent.reshape(gx, count // gx, dim), ("gz", "gh"), 0, 0, tiled=True
        ).reshape(count, dim)
        return reorder(row(tok_order), gt).reshape(tx, ty, tz, dim)

    return local


def solution(mesh):
    gx, gy = mesh.shape["gx"], mesh.shape["gy"]
    halved = Mesh(mesh.devices.reshape(NZ, gx // NZ, gy), ("gz", "gh", "gy"))
    tile = P(("gz", "gh"), "gy", None, None)
    return jax.shard_map(
        make_local(NZ, gx // NZ, gy),
        mesh=halved,
        in_specs=(tile, tile) + (P(),) * 9,
        out_specs=tile,
        check_vma=False,
    )
```

```python
import jax
import jax.numpy as jnp
import numpy as np
from jax import lax
from jax.experimental import pallas as pl
from jax.experimental.pallas import tpu as pltpu
from jax.sharding import Mesh
from jax.sharding import PartitionSpec as P

HEADS = 8
NZ = 2
EPS = 1e-05
F32 = jnp.float32
BF16 = jnp.bfloat16
VMEM_LIMIT = 56 * 1024 * 1024


def dot(a, b):
    return jnp.dot(a, b, preferred_element_type=F32)


def dot_t(a, b):
    return lax.dot_general(a, b, (((1,), (1,)), ((), ())), preferred_element_type=F32)


def dot_lt(a, b):
    return lax.dot_general(a, b, (((0,), (0,)), ((), ())), preferred_element_type=F32)


def one_hot(target):
    size = target.shape[1]
    rows = lax.broadcasted_iota(jnp.int32, (size, size), 0)
    return jnp.where(rows == target, 1.0, 0.0).astype(BF16)


def standardize(x):
    centred = x - jnp.mean(x, -1, keepdims=True)
    inv = lax.rsqrt(jnp.mean(centred * centred, -1, keepdims=True) + EPS)
    return centred * inv, inv


def norm_back(x, gain, grad):
    unit, inv = standardize(x)
    scaled = grad * gain
    return inv * (
        scaled
        - jnp.mean(scaled, -1, keepdims=True)
        - unit * jnp.mean(scaled * unit, -1, keepdims=True)
    )


def group_of(length):
    return 4 if length * 4 <= 256 and HEADS % 4 == 0 else 2


def spread(block, count):
    width = block.shape[1] // count
    lane = lax.broadcasted_iota(jnp.int32, block.shape, 1)
    zero = jnp.zeros_like(block)
    return jnp.concatenate(
        [
            jnp.where((lane >= i * width) & (lane < (i + 1) * width), block, zero)
            for i in range(count)
        ],
        0,
    )


def gather(block, count):
    rows = block.shape[0] // count
    width = block.shape[1] // count
    lane = lax.broadcasted_iota(jnp.int32, (rows, block.shape[1]), 1)
    result = block[:rows]
    for i in range(1, count):
        result = jnp.where(lane >= i * width, block[i * rows : (i + 1) * rows], result)
    return result


class Blocks:
    def __init__(self, count, dim, length):
        self.group = group_of(length)
        self.dim = dim
        self.width = dim // HEADS * self.group
        self.scale = (dim // HEADS) ** -0.5
        self.items = [
            (slice(i * length, (i + 1) * length), j)
            for i in range(count // length)
            for j in range(HEADS // self.group)
        ]

    def lanes(self, j, part=0):
        return slice(part * self.dim + j * self.width, part * self.dim + (j + 1) * self.width)

    def q_wide(self, qkv, rows, j):
        return spread(qkv[rows, self.lanes(j)] * jnp.array(self.scale, BF16), self.group)


def softmax_rows(scores):
    exponent = jnp.exp(scores - jnp.max(scores, 0, keepdims=True))
    return exponent * (1.0 / jnp.sum(exponent, 0, keepdims=True))


def attend(blocks, qkv, mixed, keep=None):
    scores = [
        dot_t(qkv[rows, blocks.lanes(j, 1)], blocks.q_wide(qkv, rows, j))
        for rows, j in blocks.items
    ]
    lows = []
    for i, score in enumerate(scores):
        probs = softmax_rows(score)
        if keep is not None:
            keep[i] = probs
        lows.append(probs.astype(BF16))
    for (rows, j), low in zip(blocks.items, lows):
        out = dot_lt(low, qkv[rows, blocks.lanes(j, 2)])
        mixed[rows, blocks.lanes(j)] = gather(out, blocks.group).astype(BF16)


def attend_back(blocks, qkv, grad, grad_qkv, kept=None):
    probs_all, g_probs_all = [], []
    for i, (rows, j) in enumerate(blocks.items):
        if kept is None:
            probs_all.append(dot_t(qkv[rows, blocks.lanes(j, 1)], blocks.q_wide(qkv, rows, j)))
        g_wide = spread(grad[rows, blocks.lanes(j)], blocks.group)
        g_probs_all.append(dot_t(qkv[rows, blocks.lanes(j, 2)], g_wide))
    lows, g_scores_all = [], []
    for i, g_probs in enumerate(g_probs_all):
        probs = softmax_rows(probs_all[i]) if kept is None else kept[i]
        weighted = probs * g_probs
        total = jnp.sum(weighted, 0, keepdims=True)
        g_scores_all.append((weighted - probs * total).astype(BF16))
        lows.append(probs.astype(BF16))
    for (rows, j), low, g_scores in zip(blocks.items, lows, g_scores_all):
        g_q = gather(dot_lt(g_scores, qkv[rows, blocks.lanes(j, 1)]), blocks.group)
        grad_qkv[rows, blocks.lanes(j)] = (g_q * blocks.scale).astype(BF16)
        g_k = dot(g_scores, blocks.q_wide(qkv, rows, j))
        grad_qkv[rows, blocks.lanes(j, 1)] = g_k.astype(BF16)
        g_v = dot(low, spread(grad[rows, blocks.lanes(j)], blocks.group))
        grad_qkv[rows, blocks.lanes(j, 2)] = g_v.astype(BF16)


def fetch(sems, *pairs):
    copies = [
        pltpu.make_async_copy(source, target, sems.at[i])
        for i, (source, target) in enumerate(pairs)
    ]
    for copy in copies:
        copy.start()
    return copies


def project_qkv(normed, w_qkv, qkv):
    dim = w_qkv.shape[0]
    for j in range(3):
        cols = slice(j * dim, (j + 1) * dim)
        qkv[:, cols] = dot(normed[...], w_qkv[:, cols]).astype(BF16)


def unpack_body(slab_target, target, packed, out, rows):
    slab = slab_target.shape[1]
    blocks = out.shape[1] // 128
    step = slab // blocks
    pick = one_hot(slab_target[...])
    for s in range(packed.shape[0] // slab):
        found = dot(pick, packed[s * slab : (s + 1) * slab, :]).astype(BF16)
        for c in range(blocks):
            rows[s * step : (s + 1) * step, c * 128 : (c + 1) * 128] = found[
                c * step : (c + 1) * step
            ]
    out[...] = dot(one_hot(target[...]), rows[...]).astype(BF16)


def pack_body(slab_target, target, source, packed, rows):
    slab = slab_target.shape[1]
    blocks = source.shape[1] // 128
    step = slab // blocks
    rows[...] = dot(one_hot(target[...]), source[...]).astype(BF16)
    pick = one_hot(slab_target[...])
    for s in range(packed.shape[0] // slab):
        found = jnp.concatenate(
            [rows[s * step : (s + 1) * step, c * 128 : (c + 1) * 128] for c in range(blocks)], 0
        )
        packed[s * slab : (s + 1) * slab, :] = dot(pick, found).astype(BF16)


def x_forward_body(
    target, tok, gain, w_qkv_hbm, w_out_hbm, sent, qkv, normed, mixed, w_qkv, w_out, sems
):
    copies = fetch(sems, (w_qkv_hbm, w_qkv), (w_out_hbm, w_out))
    blocks, lines, part, dim = tok.shape
    length = blocks * part
    for i in range(lines):
        x = tok[:, i].reshape(length, dim).astype(F32)
        unit, _ = standardize(x)
        normed[i * length : (i + 1) * length, :] = (unit * gain[...]).astype(BF16)
    copies[0].wait()
    project_qkv(normed, w_qkv, qkv)
    attend(Blocks(normed.shape[0], dim, length), qkv, mixed)
    copies[1].wait()
    out = dot(mixed[...], w_out[...])
    for i in range(lines):
        rows = slice(i * length, (i + 1) * length)
        x = tok[:, i].reshape(length, dim).astype(F32)
        normed[rows, :] = (x + out[rows]).astype(BF16)
    sent[...] = dot(one_hot(target[...]), normed[...]).astype(BF16)


def middle_body(
    pieces, length, to_line, to_sent, s1_in, cot_other, *refs
):
    (
        gain_y, gain_m, w_qkv_hbm, w_out_hbm, w_up_hbm, w_down_hbm, sent,
        s1, cot, normed, qkv, mixed, s2, probs, acc, grad, grad_qkv,
        w_qkv, w_out, w_up, w_down, sems,
    ) = refs[pieces:]
    cot_own = refs[:pieces]
    copies = fetch(
        sems, (w_qkv_hbm, w_qkv), (w_out_hbm, w_out), (w_up_hbm, w_up), (w_down_hbm, w_down)
    )
    count, dim = s1.shape
    hidden = w_up.shape[1]
    part = length // pieces
    lines = count // length
    s1[...] = dot(one_hot(to_line[...]), s1_in[...]).astype(BF16)
    unit, _ = standardize(s1[...].astype(F32))
    normed[...] = (unit * gain_y[...]).astype(BF16)
    for i in range(lines):
        for k in range(pieces):
            source = cot_own[k] if i < lines // 2 else cot_other
            start = (i if i < lines // 2 else (k - 1) * (lines // 2) + i) * part
            cot[i * length + k * part : i * length + (k + 1) * part, :] = source[
                start : start + part, :
            ]
    copies[0].wait()
    project_qkv(normed, w_qkv, qkv)
    blocks = Blocks(count, dim, length)
    attend(blocks, qkv, mixed, probs)
    copies[1].wait()
    low = (s1[...].astype(F32) + dot(mixed[...], w_out[...])).astype(BF16)
    s2[...] = low
    unit, _ = standardize(low.astype(F32))
    normed[...] = (unit * gain_m[...]).astype(BF16)

    copies[2].wait()
    copies[3].wait()
    chunk = 512 if hidden % 512 == 0 else hidden
    c0 = 0.7978845608028654
    c1 = 0.044715
    for c in range(hidden // chunk):
        cols = slice(c * chunk, (c + 1) * chunk)
        pre = dot(normed[...], w_up[:, cols])
        g_act = dot_t(cot[...], w_down[cols, :]).astype(BF16).astype(F32)
        square = pre * pre
        half = 0.5 * jnp.tanh(pre * (c0 + (c0 * c1) * square)) + 0.5
        slope = half + pre * (half - half * half) * (2 * c0 + (6 * c0 * c1) * square)
        g_pre = (g_act * slope).astype(BF16)
        part_sum = dot_t(g_pre, w_up[:, cols])
        acc[...] = part_sum if c == 0 else acc[...] + part_sum

    back = norm_back(s2[...].astype(F32), gain_m[...], acc[...])
    cot[...] = (cot[...].astype(F32) + back).astype(BF16)
    grad[...] = dot_t(cot[...], w_out[...]).astype(BF16)
    attend_back(blocks, qkv, grad, grad_qkv, probs)
    acc[...] = dot_t(grad_qkv[...], w_qkv[...])
    back = norm_back(s1[...].astype(F32), gain_y[...], acc[...])
    normed[...] = (cot[...].astype(F32) + back).astype(BF16)
    sent[...] = dot(one_hot(to_sent[...]), normed[...]).astype(BF16)


def x_back_body(
    to_line, g1_in, tok_hbm, qkv_hbm, gain, w_qkv_hbm, w_out_hbm, sent,
    g1, grad, grad_qkv, acc, tok, qkv, w_qkv, w_out, sems,
):
    copies = fetch(
        sems, (w_out_hbm, w_out), (qkv_hbm, qkv), (w_qkv_hbm, w_qkv), (tok_hbm, tok)
    )
    blocks, lines, part, dim = tok.shape
    length = blocks * part
    g1[...] = dot(one_hot(to_line[...]), g1_in[...]).astype(BF16)
    copies[0].wait()
    grad[...] = dot_t(g1[...], w_out[...]).astype(BF16)
    copies[1].wait()
    attend_back(Blocks(g1.shape[0], dim, length), qkv, grad, grad_qkv)
    copies[2].wait()
    copies[3].wait()
    acc[...] = dot_t(grad_qkv[...], w_qkv[...])
    for i in range(lines):
        rows = slice(i * length, (i + 1) * length)
        x = tok[:, i].reshape(length, dim).astype(F32)
        total = g1[rows, :].astype(F32) + norm_back(x, gain[...], acc[rows, :])
        sent[:, i] = total.astype(BF16).reshape(blocks, part, dim)


def call(body, name, outs, scratch, args, in_hbm=(), flops=10**9):
    vmem = pl.BlockSpec(memory_space=pltpu.VMEM)
    return pl.pallas_call(
        body,
        out_shape=outs,
        in_specs=[
            pl.BlockSpec(memory_space=pl.ANY) if i in in_hbm else vmem for i in range(len(args))
        ],
        scratch_shapes=scratch,
        compiler_params=pltpu.CompilerParams(vmem_limit_bytes=VMEM_LIMIT),
        cost_estimate=pl.CostEstimate(flops=flops, bytes_accessed=4000000, transcendentals=0),
        name=name,
    )(*args)


def inverse(order):
    result = np.empty_like(order)
    result[order] = np.arange(order.size, dtype=order.dtype)
    return result


def row(order):
    return np.asarray(order, np.int32).reshape(1, -1)


def make_local(gh, gy):
    gx = NZ * gh

    def local(
        tokens, cotangent, gain_x, w_qkv_x, w_out_x, gain_y, w_qkv_y, w_out_y, gain_mlp, w_up,
        w_down,
    ):
        tx, ty, tz, dim = tokens.shape
        hidden = w_up.shape[1]
        count = tx * ty * tz
        y_lines = ty // gh
        own = tx // gy
        x_lines = tz * own
        len_x, len_y = tx * gx, ty * gy
        half, mine = lax.axis_index("gz"), lax.axis_index("gy")

        def vm(shape, dtype=BF16):
            return pltpu.VMEM(shape, dtype)

        def pick(options, index):
            table = jnp.asarray(np.stack([row(o) for o in options]))
            return lax.dynamic_index_in_dim(table, index, keepdims=False)

        tile_row = np.arange(count).reshape(tx, ty, tz)
        tok_order = tile_row.reshape(tx, gh, y_lines, tz).transpose(3, 1, 2, 0).reshape(-1)
        cot_orders = []
        for z in range(NZ):
            for g in range(gy):
                cut = tile_row.reshape(gy, own, ty, tz).transpose(0, 3, 1, 2)
                cut = cut[[g ^ k for k in range(gy)]][:, [z, 1 - z]]
                cot_orders.append(cut.reshape(-1))
        line_row = np.arange(count).reshape(y_lines, NZ, gh, gy, own)
        out_orders = [
            line_row[:, [z, 1 - z]].transpose(3, 2, 0, 1, 4).reshape(-1) for z in range(NZ)
        ]
        come_row = np.arange(count).reshape(gy, gh * y_lines, x_lines)
        y_orders = [
            come_row[[g ^ k for k in range(gy)]].transpose(2, 0, 1).reshape(-1)
            for g in range(gy)
        ]
        lane_blocks = dim // 128
        slab = 32 * tz * lane_blocks
        slab_order = np.arange(slab).reshape(32, lane_blocks, tz).transpose(1, 0, 2).reshape(-1)

        def packed(array):
            split = array.reshape(tx, ty, tz, lane_blocks, 128).transpose(0, 1, 3, 2, 4)
            return split.reshape(count * lane_blocks, 128)

        def unpack(array, target):
            return call(
                unpack_body, "unpack", flat, [vm((count, dim))],
                (row(inverse(slab_order)), target, packed(array)),
            )

        flat = jax.ShapeDtypeStruct((count, dim), BF16)
        gain_x, gain_y, gain_mlp = (g.reshape(1, dim) for g in (gain_x, gain_y, gain_mlp))

        tok_sent = unpack(tokens, row(inverse(tok_order)))
        tok_x = lax.all_to_all(
            tok_sent.reshape(gx, count // gx, dim), ("gz", "gh"), 0, 0, tiled=True
        ).reshape(gx, y_lines, tx, dim)

        cot_sent = unpack(
            cotangent, pick([inverse(o) for o in cot_orders], half * gy + mine)
        ).reshape(gy, count // gy, dim)
        cot_own = [cot_sent[0]] + [
            lax.ppermute(cot_sent[k], "gy", [(i, i ^ k) for i in range(gy)])
            for k in range(1, gy)
        ]
        cot_other = lax.ppermute(
            jnp.concatenate([piece[piece.shape[0] // 2 :] for piece in cot_own], 0),
            "gz",
            [(0, 1), (1, 0)],
        )

        sent, qkv_x = call(
            x_forward_body,
            "x_forward",
            (flat, jax.ShapeDtypeStruct((count, 3 * dim), BF16)),
            [
                vm((count, dim)),
                vm((count, dim)),
                vm((dim, 3 * dim)),
                vm((dim, dim)),
                pltpu.SemaphoreType.DMA((2,)),
            ],
            (pick([inverse(o) for o in out_orders], half), tok_x, gain_x, w_qkv_x, w_out_x),
            in_hbm=(3, 4),
            flops=3 * 10**9,
        )
        s1_y = lax.all_to_all(
            sent.reshape(gh * gy, count // (gh * gy), dim), ("gy", "gh"), 0, 0, tiled=True
        ).reshape(count, dim)

        group = group_of(len_y)
        g1_sent = call(
            lambda *refs: middle_body(gy, len_y, *refs),
            "middle",
            flat,
            [
                vm((count, dim)),
                vm((count, dim)),
                vm((count, dim)),
                vm((count, 3 * dim)),
                vm((count, dim)),
                vm((count, dim)),
                vm((x_lines * HEADS // group, len_y, group * len_y), F32),
                vm((count, dim), F32),
                vm((count, dim)),
                vm((count, 3 * dim)),
                vm((dim, 3 * dim)),
                vm((dim, dim)),
                vm((dim, hidden)),
                vm((hidden, dim)),
                pltpu.SemaphoreType.DMA((4,)),
            ],
            (
                pick([inverse(o) for o in y_orders], mine),
                pick(y_orders, mine),
                s1_y,
                cot_other,
                *cot_own,
                gain_y, gain_mlp, w_qkv_y, w_out_y, w_up, w_down,
            ),
            in_hbm=tuple(range(gy + 6, gy + 10)),
            flops=9 * 10**9,
        )
        g1_x = lax.all_to_all(
            g1_sent.reshape(gh * gy, count // (gh * gy), dim), ("gy", "gh"), 0, 0, tiled=True
        ).reshape(count, dim)

        gt_sent = call(
            x_back_body,
            "x_back",
            jax.ShapeDtypeStruct(tok_x.shape, BF16),
            [
                vm((count, dim)),
                vm((count, dim)),
                vm((count, 3 * dim)),
                vm((count, dim), F32),
                vm(tok_x.shape),
                vm((count, 3 * dim)),
                vm((dim, 3 * dim)),
                vm((dim, dim)),
                pltpu.SemaphoreType.DMA((4,)),
            ],
            (pick(out_orders, half), g1_x, tok_x, qkv_x, gain_x, w_qkv_x, w_out_x),
            in_hbm=(2, 3, 5, 6),
            flops=3 * 10**9,
        )
        gt = lax.all_to_all(
            gt_sent.reshape(gx, count // gx, dim), ("gz", "gh"), 0, 0, tiled=True
        ).reshape(count, dim)
        out = call(
            pack_body,
            "pack",
            jax.ShapeDtypeStruct((count * lane_blocks, 128), BF16),
            [vm((count, dim))],
            (row(slab_order), row(tok_order), gt),
        )
        split = out.reshape(tx, ty, lane_blocks, tz, 128).transpose(0, 1, 3, 2, 4)
        return split.reshape(tx, ty, tz, dim)

    return local


def solution(mesh):
    gx, gy = mesh.shape["gx"], mesh.shape["gy"]
    halved = Mesh(mesh.devices.reshape(NZ, gx // NZ, gy), ("gz", "gh", "gy"))
    tile = P(("gz", "gh"), "gy", None, None)
    return jax.shard_map(
        make_local(gx // NZ, gy),
        mesh=halved,
        in_specs=(tile, tile) + (P(),) * 9,
        out_specs=tile,
        check_vma=False,
    )
```

```python
import jax
import jax.numpy as jnp
import numpy as np
from jax import lax
from jax.experimental import pallas as pl
from jax.experimental.pallas import tpu as pltpu
from jax.sharding import Mesh
from jax.sharding import PartitionSpec as P

HEADS = 8
NZ = 2
EPS = 1e-05
F32 = jnp.float32
BF16 = jnp.bfloat16
MIB = 1024 * 1024


def dot(a, b):
    return jnp.dot(a, b, preferred_element_type=F32)


def dot_t(a, b):
    return lax.dot_general(a, b, (((1,), (1,)), ((), ())), preferred_element_type=F32)


def dot_lt(a, b):
    return lax.dot_general(a, b, (((0,), (0,)), ((), ())), preferred_element_type=F32)


def one_hot(target):
    size = target.shape[1]
    rows = lax.broadcasted_iota(jnp.int32, (size, size), 0)
    return jnp.where(rows == target, 1.0, 0.0).astype(BF16)


def standardize(x):
    centred = x - jnp.mean(x, -1, keepdims=True)
    inv = lax.rsqrt(jnp.mean(centred * centred, -1, keepdims=True) + EPS)
    return centred * inv, inv


def norm_back(x, gain, grad):
    unit, inv = standardize(x)
    scaled = grad * gain
    return inv * (
        scaled
        - jnp.mean(scaled, -1, keepdims=True)
        - unit * jnp.mean(scaled * unit, -1, keepdims=True)
    )


def group_of(length):
    return 4 if length * 4 <= 256 and HEADS % 4 == 0 else 2


def spread(block, count):
    width = block.shape[1] // count
    lane = lax.broadcasted_iota(jnp.int32, block.shape, 1)
    zero = jnp.zeros_like(block)
    return jnp.concatenate(
        [
            jnp.where((lane >= i * width) & (lane < (i + 1) * width), block, zero)
            for i in range(count)
        ],
        0,
    )


def gather(block, count):
    rows = block.shape[0] // count
    width = block.shape[1] // count
    lane = lax.broadcasted_iota(jnp.int32, (rows, block.shape[1]), 1)
    result = block[:rows]
    for i in range(1, count):
        result = jnp.where(lane >= i * width, block[i * rows : (i + 1) * rows], result)
    return result


class Blocks:
    def __init__(self, count, dim, length):
        self.group = group_of(length)
        self.dim = dim
        self.width = dim // HEADS * self.group
        self.scale = (dim // HEADS) ** -0.5
        self.items = [
            (slice(i * length, (i + 1) * length), j)
            for i in range(count // length)
            for j in range(HEADS // self.group)
        ]

    def lanes(self, j, part=0):
        return slice(part * self.dim + j * self.width, part * self.dim + (j + 1) * self.width)

    def q_wide(self, qkv, rows, j):
        return spread(qkv[rows, self.lanes(j)] * jnp.array(self.scale, BF16), self.group)


def softmax_rows(scores):
    exponent = jnp.exp(scores - jnp.max(scores, 0, keepdims=True))
    return exponent * (1.0 / jnp.sum(exponent, 0, keepdims=True))


def attend(blocks, qkv, mixed, keep=None):
    scores = [
        dot_t(qkv[rows, blocks.lanes(j, 1)], blocks.q_wide(qkv, rows, j))
        for rows, j in blocks.items
    ]
    lows = []
    for i, score in enumerate(scores):
        probs = softmax_rows(score)
        if keep is not None:
            keep[i] = probs
        lows.append(probs.astype(BF16))
    for (rows, j), low in zip(blocks.items, lows):
        out = dot_lt(low, qkv[rows, blocks.lanes(j, 2)])
        mixed[rows, blocks.lanes(j)] = gather(out, blocks.group).astype(BF16)


def attend_back(blocks, qkv, grad, grad_qkv, kept=None):
    probs_all, g_probs_all = [], []
    for i, (rows, j) in enumerate(blocks.items):
        if kept is None:
            probs_all.append(dot_t(qkv[rows, blocks.lanes(j, 1)], blocks.q_wide(qkv, rows, j)))
        g_wide = spread(grad[rows, blocks.lanes(j)], blocks.group)
        g_probs_all.append(dot_t(qkv[rows, blocks.lanes(j, 2)], g_wide))
    lows, g_scores_all = [], []
    for i, g_probs in enumerate(g_probs_all):
        probs = softmax_rows(probs_all[i]) if kept is None else kept[i]
        weighted = probs * g_probs
        total = jnp.sum(weighted, 0, keepdims=True)
        g_scores_all.append((weighted - probs * total).astype(BF16))
        lows.append(probs.astype(BF16))
    for (rows, j), low, g_scores in zip(blocks.items, lows, g_scores_all):
        g_q = gather(dot_lt(g_scores, qkv[rows, blocks.lanes(j, 1)]), blocks.group)
        grad_qkv[rows, blocks.lanes(j)] = (g_q * blocks.scale).astype(BF16)
        g_k = dot(g_scores, blocks.q_wide(qkv, rows, j))
        grad_qkv[rows, blocks.lanes(j, 1)] = g_k.astype(BF16)
        g_v = dot(low, spread(grad[rows, blocks.lanes(j)], blocks.group))
        grad_qkv[rows, blocks.lanes(j, 2)] = g_v.astype(BF16)


def fetch(sems, *pairs):
    copies = [
        pltpu.make_async_copy(source, target, sems.at[i])
        for i, (source, target) in enumerate(pairs)
    ]
    for copy in copies:
        copy.start()
    return copies


def project_qkv(normed, w_qkv, qkv):
    dim = w_qkv.shape[0]
    for j in range(3):
        cols = slice(j * dim, (j + 1) * dim)
        qkv[:, cols] = dot(normed[...], w_qkv[:, cols]).astype(BF16)


def unpack_body(slab_target, target, packed, out, rows):
    slab = slab_target.shape[1]
    blocks = out.shape[1] // 128
    step = slab // blocks
    pick = one_hot(slab_target[...])
    for s in range(packed.shape[0] // slab):
        found = dot(pick, packed[s * slab : (s + 1) * slab, :]).astype(BF16)
        for c in range(blocks):
            rows[s * step : (s + 1) * step, c * 128 : (c + 1) * 128] = found[
                c * step : (c + 1) * step
            ]
    out[...] = dot(one_hot(target[...]), rows[...]).astype(BF16)


def pack_body(slab_target, target, source, packed, rows):
    slab = slab_target.shape[1]
    blocks = source.shape[1] // 128
    step = slab // blocks
    rows[...] = dot(one_hot(target[...]), source[...]).astype(BF16)
    pick = one_hot(slab_target[...])
    for s in range(packed.shape[0] // slab):
        found = jnp.concatenate(
            [rows[s * step : (s + 1) * step, c * 128 : (c + 1) * 128] for c in range(blocks)], 0
        )
        packed[s * slab : (s + 1) * slab, :] = dot(pick, found).astype(BF16)


def x_forward_body(
    target, tok, gain, w_qkv_hbm, w_out_hbm, sent, qkv, normed, mixed, w_qkv, w_out, sems
):
    copies = fetch(sems, (w_qkv_hbm, w_qkv), (w_out_hbm, w_out))
    blocks, lines, part, dim = tok.shape
    length = blocks * part
    for i in range(lines):
        x = tok[:, i].reshape(length, dim).astype(F32)
        unit, _ = standardize(x)
        normed[i * length : (i + 1) * length, :] = (unit * gain[...]).astype(BF16)
    copies[0].wait()
    project_qkv(normed, w_qkv, qkv)
    attend(Blocks(normed.shape[0], dim, length), qkv, mixed)
    copies[1].wait()
    out = dot(mixed[...], w_out[...])
    for i in range(lines):
        rows = slice(i * length, (i + 1) * length)
        x = tok[:, i].reshape(length, dim).astype(F32)
        normed[rows, :] = (x + out[rows]).astype(BF16)
    sent[...] = dot(one_hot(target[...]), normed[...]).astype(BF16)


def middle_body(
    pieces, length, to_line, to_sent, s1_in, cot_other_a, cot_other_b, *refs
):
    (
        gain_y, gain_m, w_qkv_hbm, w_out_hbm, w_up_hbm, w_down_hbm, sent,
        s1, cot, normed, qkv, mixed, s2, probs, acc, grad, grad_qkv,
        w_qkv, w_out, w_up, w_down, sems,
    ) = refs[pieces:]
    cot_own = refs[:pieces]
    copies = fetch(
        sems, (w_qkv_hbm, w_qkv), (w_out_hbm, w_out), (w_up_hbm, w_up), (w_down_hbm, w_down)
    )
    count, dim = s1.shape
    hidden = w_up.shape[1]
    part = length // pieces
    lines = count // length
    s1[...] = dot(one_hot(to_line[...]), s1_in[...]).astype(BF16)
    unit, _ = standardize(s1[...].astype(F32))
    normed[...] = (unit * gain_y[...]).astype(BF16)
    for i in range(lines):
        for k in range(pieces):
            if i < lines // 2:
                source, start = cot_own[k], i * part
            else:
                source = cot_other_a if k < pieces // 2 else cot_other_b
                start = (k % (pieces // 2) * (lines // 2) + i - lines // 2) * part
            cot[i * length + k * part : i * length + (k + 1) * part, :] = source[
                start : start + part, :
            ]
    copies[0].wait()
    project_qkv(normed, w_qkv, qkv)
    blocks = Blocks(count, dim, length)
    attend(blocks, qkv, mixed, probs)
    copies[1].wait()
    low = (s1[...].astype(F32) + dot(mixed[...], w_out[...])).astype(BF16)
    s2[...] = low
    unit, _ = standardize(low.astype(F32))
    normed[...] = (unit * gain_m[...]).astype(BF16)

    copies[2].wait()
    copies[3].wait()
    chunk = 512 if hidden % 512 == 0 else hidden
    c0 = 0.7978845608028654
    c1 = 0.044715
    for c in range(hidden // chunk):
        cols = slice(c * chunk, (c + 1) * chunk)
        pre = dot(normed[...], w_up[:, cols])
        g_act = dot_t(cot[...], w_down[cols, :]).astype(BF16).astype(F32)
        square = pre * pre
        half = 0.5 * jnp.tanh(pre * (c0 + (c0 * c1) * square)) + 0.5
        slope = half + pre * (half - half * half) * (2 * c0 + (6 * c0 * c1) * square)
        g_pre = (g_act * slope).astype(BF16)
        part_sum = dot_t(g_pre, w_up[:, cols])
        acc[...] = part_sum if c == 0 else acc[...] + part_sum

    back = norm_back(s2[...].astype(F32), gain_m[...], acc[...])
    cot[...] = (cot[...].astype(F32) + back).astype(BF16)
    grad[...] = dot_t(cot[...], w_out[...]).astype(BF16)
    attend_back(blocks, qkv, grad, grad_qkv, probs)
    acc[...] = dot_t(grad_qkv[...], w_qkv[...])
    back = norm_back(s1[...].astype(F32), gain_y[...], acc[...])
    normed[...] = (cot[...].astype(F32) + back).astype(BF16)
    sent[...] = dot(one_hot(to_sent[...]), normed[...]).astype(BF16)


def x_back_body(
    to_line, g1_in, tok_hbm, qkv_hbm, gain, w_qkv_hbm, w_out_hbm, sent,
    g1, grad, grad_qkv, acc, tok, qkv, w_qkv, w_out, sems,
):
    copies = fetch(
        sems, (w_out_hbm, w_out), (qkv_hbm, qkv), (w_qkv_hbm, w_qkv), (tok_hbm, tok)
    )
    blocks, lines, part, dim = tok.shape
    length = blocks * part
    g1[...] = dot(one_hot(to_line[...]), g1_in[...]).astype(BF16)
    copies[0].wait()
    grad[...] = dot_t(g1[...], w_out[...]).astype(BF16)
    copies[1].wait()
    attend_back(Blocks(g1.shape[0], dim, length), qkv, grad, grad_qkv)
    copies[2].wait()
    copies[3].wait()
    acc[...] = dot_t(grad_qkv[...], w_qkv[...])
    for i in range(lines):
        rows = slice(i * length, (i + 1) * length)
        x = tok[:, i].reshape(length, dim).astype(F32)
        total = g1[rows, :].astype(F32) + norm_back(x, gain[...], acc[rows, :])
        sent[:, i] = total.astype(BF16).reshape(blocks, part, dim)


def call(body, name, outs, scratch, args, vmem_mib, in_hbm=(), flops=10**9):
    vmem = pl.BlockSpec(memory_space=pltpu.VMEM)
    return pl.pallas_call(
        body,
        out_shape=outs,
        in_specs=[
            pl.BlockSpec(memory_space=pl.ANY) if i in in_hbm else vmem for i in range(len(args))
        ],
        scratch_shapes=scratch,
        compiler_params=pltpu.CompilerParams(vmem_limit_bytes=vmem_mib * MIB),
        cost_estimate=pl.CostEstimate(flops=flops, bytes_accessed=4000000, transcendentals=0),
        name=name,
    )(*args)


def inverse(order):
    result = np.empty_like(order)
    result[order] = np.arange(order.size, dtype=order.dtype)
    return result


def row(order):
    return np.asarray(order, np.int32).reshape(1, -1)


def make_local(gh, gy):
    gx = NZ * gh

    def local(
        tokens, cotangent, gain_x, w_qkv_x, w_out_x, gain_y, w_qkv_y, w_out_y, gain_mlp, w_up,
        w_down,
    ):
        tx, ty, tz, dim = tokens.shape
        hidden = w_up.shape[1]
        count = tx * ty * tz
        y_lines = ty // gh
        own = tx // gy
        x_lines = tz * own
        len_x, len_y = tx * gx, ty * gy
        half, mine = lax.axis_index("gz"), lax.axis_index("gy")

        def vm(shape, dtype=BF16):
            return pltpu.VMEM(shape, dtype)

        def pick(options, index):
            table = jnp.asarray(np.stack([row(o) for o in options]))
            return lax.dynamic_index_in_dim(table, index, keepdims=False)

        tile_row = np.arange(count).reshape(tx, ty, tz)
        tok_order = tile_row.reshape(tx, gh, y_lines, tz).transpose(3, 1, 2, 0).reshape(-1)
        cot_orders = []
        for z in range(NZ):
            for g in range(gy):
                cut = tile_row.reshape(gy, own, ty, tz).transpose(0, 3, 1, 2)
                cut = cut[[g ^ k for k in range(gy)]][:, [z, 1 - z]]
                cot_orders.append(cut.reshape(-1))
        line_row = np.arange(count).reshape(y_lines, NZ, gh, gy, own)
        out_orders = [
            line_row[:, [z, 1 - z]].transpose(3, 2, 0, 1, 4).reshape(-1) for z in range(NZ)
        ]
        come_row = np.arange(count).reshape(gy, gh * y_lines, x_lines)
        y_orders = [
            come_row[[g ^ k for k in range(gy)]].transpose(2, 0, 1).reshape(-1)
            for g in range(gy)
        ]
        lane_blocks = dim // 128
        slab = 32 * tz * lane_blocks
        slab_order = np.arange(slab).reshape(32, lane_blocks, tz).transpose(1, 0, 2).reshape(-1)

        def packed(array):
            split = array.reshape(tx, ty, tz, lane_blocks, 128).transpose(0, 1, 3, 2, 4)
            return split.reshape(count * lane_blocks, 128)

        def unpack(array, target):
            return call(
                unpack_body, "unpack", flat, [vm((count, dim))],
                (row(inverse(slab_order)), target, packed(array)),
                vmem_mib=10,
            )

        flat = jax.ShapeDtypeStruct((count, dim), BF16)
        gain_x, gain_y, gain_mlp = (g.reshape(1, dim) for g in (gain_x, gain_y, gain_mlp))

        tok_sent = unpack(tokens, row(inverse(tok_order)))
        tok_x = lax.all_to_all(
            tok_sent.reshape(gx, count // gx, dim), ("gz", "gh"), 0, 0, tiled=True
        ).reshape(gx, y_lines, tx, dim)

        cot_sent = unpack(
            cotangent, pick([inverse(o) for o in cot_orders], half * gy + mine)
        ).reshape(gy, count // gy, dim)
        cot_own = [cot_sent[0]] + [
            lax.ppermute(cot_sent[k], "gy", [(i, i ^ k) for i in range(gy)])
            for k in range(1, gy)
        ]
        parts = [
            jnp.concatenate([piece[piece.shape[0] // 2 :] for piece in pieces], 0)
            for pieces in (cot_own[: gy // 2], cot_own[gy // 2 :])
        ]
        *parts, tok_x = lax.optimization_barrier((*parts, tok_x))
        cot_other = [lax.ppermute(part, "gz", [(0, 1), (1, 0)]) for part in parts]

        sent, qkv_x = call(
            x_forward_body,
            "x_forward",
            (flat, jax.ShapeDtypeStruct((count, 3 * dim), BF16)),
            [
                vm((count, dim)),
                vm((count, dim)),
                vm((dim, 3 * dim)),
                vm((dim, dim)),
                pltpu.SemaphoreType.DMA((2,)),
            ],
            (pick([inverse(o) for o in out_orders], half), tok_x, gain_x, w_qkv_x, w_out_x),
            vmem_mib=52,
            in_hbm=(3, 4),
            flops=3 * 10**9,
        )
        sent, cot_other[0] = lax.optimization_barrier((sent, cot_other[0]))
        s1_y = lax.all_to_all(
            sent.reshape(gh * gy, count // (gh * gy), dim), ("gy", "gh"), 0, 0, tiled=True
        ).reshape(count, dim)

        group = group_of(len_y)
        g1_sent = call(
            lambda *refs: middle_body(gy, len_y, *refs),
            "middle",
            flat,
            [
                vm((count, dim)),
                vm((count, dim)),
                vm((count, dim)),
                vm((count, 3 * dim)),
                vm((count, dim)),
                vm((count, dim)),
                vm((x_lines * HEADS // group, len_y, group * len_y), F32),
                vm((count, dim), F32),
                vm((count, dim)),
                vm((count, 3 * dim)),
                vm((dim, 3 * dim)),
                vm((dim, dim)),
                vm((dim, hidden)),
                vm((hidden, dim)),
                pltpu.SemaphoreType.DMA((4,)),
            ],
            (
                pick([inverse(o) for o in y_orders], mine),
                pick(y_orders, mine),
                s1_y,
                *cot_other,
                *cot_own,
                gain_y, gain_mlp, w_qkv_y, w_out_y, w_up, w_down,
            ),
            vmem_mib=52,
            in_hbm=tuple(range(gy + 7, gy + 11)),
            flops=9 * 10**9,
        )
        g1_x = lax.all_to_all(
            g1_sent.reshape(gh * gy, count // (gh * gy), dim), ("gy", "gh"), 0, 0, tiled=True
        ).reshape(count, dim)

        gt_sent = call(
            x_back_body,
            "x_back",
            jax.ShapeDtypeStruct(tok_x.shape, BF16),
            [
                vm((count, dim)),
                vm((count, dim)),
                vm((count, 3 * dim)),
                vm((count, dim), F32),
                vm(tok_x.shape),
                vm((count, 3 * dim)),
                vm((dim, 3 * dim)),
                vm((dim, dim)),
                pltpu.SemaphoreType.DMA((4,)),
            ],
            (pick(out_orders, half), g1_x, tok_x, qkv_x, gain_x, w_qkv_x, w_out_x),
            vmem_mib=52,
            in_hbm=(2, 3, 5, 6),
            flops=3 * 10**9,
        )
        gt = lax.all_to_all(
            gt_sent.reshape(gx, count // gx, dim), ("gz", "gh"), 0, 0, tiled=True
        ).reshape(count, dim)
        out = call(
            pack_body,
            "pack",
            jax.ShapeDtypeStruct((count * lane_blocks, 128), BF16),
            [vm((count, dim))],
            (row(slab_order), row(tok_order), gt),
            vmem_mib=10,
        )
        split = out.reshape(tx, ty, lane_blocks, tz, 128).transpose(0, 1, 3, 2, 4)
        return split.reshape(tx, ty, tz, dim)

    return local


def solution(mesh):
    gx, gy = mesh.shape["gx"], mesh.shape["gy"]
    halved = Mesh(mesh.devices.reshape(NZ, gx // NZ, gy), ("gz", "gh", "gy"))
    tile = P(("gz", "gh"), "gy", None, None)
    return jax.shard_map(
        make_local(gx // NZ, gy),
        mesh=halved,
        in_specs=(tile, tile) + (P(),) * 9,
        out_specs=tile,
        check_vma=False,
    )
```

```python
import jax
import jax.numpy as jnp
import numpy as np
from jax import lax
from jax.experimental import pallas as pl
from jax.experimental.pallas import tpu as pltpu
from jax.sharding import Mesh
from jax.sharding import PartitionSpec as P

HEADS = 8
NZ = 2
EPS = 1e-05
F32 = jnp.float32
BF16 = jnp.bfloat16
MIB = 1024 * 1024


def dot(a, b):
    return jnp.dot(a, b, preferred_element_type=F32)


def dot_t(a, b):
    return lax.dot_general(a, b, (((1,), (1,)), ((), ())), preferred_element_type=F32)


def dot_lt(a, b):
    return lax.dot_general(a, b, (((0,), (0,)), ((), ())), preferred_element_type=F32)


def one_hot(target):
    size = target.shape[1]
    rows = lax.broadcasted_iota(jnp.int32, (size, size), 0)
    return jnp.where(rows == target, 1.0, 0.0).astype(BF16)


def standardize(x):
    centred = x - jnp.mean(x, -1, keepdims=True)
    inv = lax.rsqrt(jnp.mean(centred * centred, -1, keepdims=True) + EPS)
    return centred * inv, inv


def norm_back(x, gain, grad):
    unit, inv = standardize(x)
    scaled = grad * gain
    return inv * (
        scaled
        - jnp.mean(scaled, -1, keepdims=True)
        - unit * jnp.mean(scaled * unit, -1, keepdims=True)
    )


def group_of(length):
    return 4 if length * 4 <= 256 and HEADS % 4 == 0 else 2


def spread(block, count):
    width = block.shape[1] // count
    lane = lax.broadcasted_iota(jnp.int32, block.shape, 1)
    zero = jnp.zeros_like(block)
    return jnp.concatenate(
        [
            jnp.where((lane >= i * width) & (lane < (i + 1) * width), block, zero)
            for i in range(count)
        ],
        0,
    )


def gather(block, count):
    rows = block.shape[0] // count
    width = block.shape[1] // count
    lane = lax.broadcasted_iota(jnp.int32, (rows, block.shape[1]), 1)
    result = block[:rows]
    for i in range(1, count):
        result = jnp.where(lane >= i * width, block[i * rows : (i + 1) * rows], result)
    return result


class Blocks:
    def __init__(self, count, dim, length):
        self.group = group_of(length)
        self.dim = dim
        self.width = dim // HEADS * self.group
        self.scale = (dim // HEADS) ** -0.5
        self.items = [
            (slice(i * length, (i + 1) * length), j)
            for i in range(count // length)
            for j in range(HEADS // self.group)
        ]

    def lanes(self, j, part=0):
        return slice(part * self.dim + j * self.width, part * self.dim + (j + 1) * self.width)

    def q_wide(self, qkv, rows, j):
        return spread(qkv[rows, self.lanes(j)] * jnp.array(self.scale, BF16), self.group)


def softmax_rows(scores):
    exponent = jnp.exp(scores - jnp.max(scores, 0, keepdims=True))
    return exponent * (1.0 / jnp.sum(exponent, 0, keepdims=True))


def attend(blocks, qkv, mixed, keep=None):
    scores = [
        dot_t(qkv[rows, blocks.lanes(j, 1)], blocks.q_wide(qkv, rows, j))
        for rows, j in blocks.items
    ]
    lows = []
    for i, score in enumerate(scores):
        probs = softmax_rows(score)
        if keep is not None:
            keep[i] = probs
        lows.append(probs.astype(BF16))
    for (rows, j), low in zip(blocks.items, lows):
        out = dot_lt(low, qkv[rows, blocks.lanes(j, 2)])
        mixed[rows, blocks.lanes(j)] = gather(out, blocks.group).astype(BF16)


def attend_back(blocks, qkv, grad, grad_qkv, kept=None):
    probs_all, g_probs_all = [], []
    for i, (rows, j) in enumerate(blocks.items):
        if kept is None:
            probs_all.append(dot_t(qkv[rows, blocks.lanes(j, 1)], blocks.q_wide(qkv, rows, j)))
        g_wide = spread(grad[rows, blocks.lanes(j)], blocks.group)
        g_probs_all.append(dot_t(qkv[rows, blocks.lanes(j, 2)], g_wide))
    lows, g_scores_all = [], []
    for i, g_probs in enumerate(g_probs_all):
        probs = softmax_rows(probs_all[i]) if kept is None else kept[i]
        weighted = probs * g_probs
        total = jnp.sum(weighted, 0, keepdims=True)
        g_scores_all.append((weighted - probs * total).astype(BF16))
        lows.append(probs.astype(BF16))
    for (rows, j), low, g_scores in zip(blocks.items, lows, g_scores_all):
        g_q = gather(dot_lt(g_scores, qkv[rows, blocks.lanes(j, 1)]), blocks.group)
        grad_qkv[rows, blocks.lanes(j)] = (g_q * blocks.scale).astype(BF16)
        g_k = dot(g_scores, blocks.q_wide(qkv, rows, j))
        grad_qkv[rows, blocks.lanes(j, 1)] = g_k.astype(BF16)
        g_v = dot(low, spread(grad[rows, blocks.lanes(j)], blocks.group))
        grad_qkv[rows, blocks.lanes(j, 2)] = g_v.astype(BF16)


def fetch(sems, *pairs):
    copies = [
        pltpu.make_async_copy(source, target, sems.at[i])
        for i, (source, target) in enumerate(pairs)
    ]
    for copy in copies:
        copy.start()
    return copies


def project_qkv(normed, w_qkv, qkv):
    dim = w_qkv.shape[0]
    for j in range(3):
        cols = slice(j * dim, (j + 1) * dim)
        qkv[:, cols] = dot(normed[...], w_qkv[:, cols]).astype(BF16)


def digits(values, *sizes):
    found = []
    for size in reversed(sizes):
        if size & (size - 1) == 0:
            found.append(values & (size - 1))
            values = values >> (size.bit_length() - 1)
        else:
            found.append(lax.rem(values, size))
            values = lax.div(values, size)
    return found[::-1]


def slab_target(depth, blocks, step):
    lane = lax.broadcasted_iota(jnp.int32, (1, step * blocks), 1)
    place, block, z = digits(lane, step // depth, blocks, depth)
    return block * step + place * depth + z


def line_target(count, tx, ty, tz, gh):
    lane = lax.broadcasted_iota(jnp.int32, (1, count), 1)
    x, r, y, z = digits(lane, tx, gh, ty // gh, tz)
    return ((z * gh + r) * (ty // gh) + y) * tx + x


def unpack_slabs(depth, packed, rows):
    blocks = rows.shape[1] // 128
    step = 32 * depth
    slab = step * blocks
    pick = one_hot(slab_target(depth, blocks, step))
    for s in range(packed.shape[0] // slab):
        found = dot(pick, packed[s * slab : (s + 1) * slab, :]).astype(BF16)
        for c in range(blocks):
            rows[s * step : (s + 1) * step, c * 128 : (c + 1) * 128] = found[
                c * step : (c + 1) * step
            ]


def unpack_tokens_body(tx, ty, tz, gh, packed, *refs):
    *outs, rows, sent = refs
    unpack_slabs(tz, packed, rows)
    target = sent if len(outs) > 1 else outs[0]
    target[...] = dot(one_hot(line_target(rows.shape[0], tx, ty, tz, gh)), rows[...]).astype(BF16)
    scatter_blocks(target, outs)


def unpack_body(tz, target, packed, out, rows):
    unpack_slabs(tz, packed, rows)
    out[...] = dot(one_hot(target[...]), rows[...]).astype(BF16)


def gx_index(count):
    return lax.axis_index("gz") * (count // NZ) + lax.axis_index("gh")


def scatter_blocks(sent, outs):
    if len(outs) == 1:
        return
    for source, out in zip(block_targets(sent, len(outs)), outs):
        out[...] = source[...]


def block_targets(whole, count):
    if count == 1:
        return [whole]
    size = whole.shape[0] // count
    me = gx_index(count)
    return [whole.at[pl.ds(pl.multiple_of((me ^ k) * size, size), size)] for k in range(count)]


def gather_blocks(blocks, whole):
    if len(blocks) == 1:
        return blocks[0]
    for block, target in zip(blocks, block_targets(whole, len(blocks))):
        target[...] = block[...]
    return whole


def pack_body(tx, ty, tz, gh, *refs):
    *parts, packed, rows, whole = refs
    source = gather_blocks(parts, whole)
    count, dim = rows.shape
    blocks = dim // 128
    step = 32 * tz
    move = one_hot(line_target(count, tx, ty, tz, gh))
    rows[...] = dot_lt(move, source[...]).astype(BF16)
    pick = one_hot(slab_target(tz, blocks, step))
    for s in range(count // step):
        found = jnp.concatenate(
            [rows[s * step : (s + 1) * step, c * 128 : (c + 1) * 128] for c in range(blocks)], 0
        )
        packed[s * step * blocks : (s + 1) * step * blocks, :] = dot_lt(pick, found).astype(BF16)


def x_forward_body(
    shape, target, gain, w_qkv_hbm, w_out_hbm, *refs
):
    *parts, sent, qkv, whole, normed, mixed, w_qkv, w_out, sems = refs
    copies = fetch(sems, (w_qkv_hbm, w_qkv), (w_out_hbm, w_out))
    tok = gather_blocks(parts, whole).reshape(shape)
    blocks, lines, part, dim = shape
    length = blocks * part
    for i in range(lines):
        x = tok[:, i].reshape(length, dim).astype(F32)
        unit, _ = standardize(x)
        normed[i * length : (i + 1) * length, :] = (unit * gain[...]).astype(BF16)
    copies[0].wait()
    project_qkv(normed, w_qkv, qkv)
    attend(Blocks(normed.shape[0], dim, length), qkv, mixed)
    copies[1].wait()
    out = dot(mixed[...], w_out[...])
    for i in range(lines):
        rows = slice(i * length, (i + 1) * length)
        x = tok[:, i].reshape(length, dim).astype(F32)
        normed[rows, :] = (x + out[rows]).astype(BF16)
    sent[...] = dot(one_hot(target[...]), normed[...]).astype(BF16)


def middle_body(
    pieces, length, to_line, to_sent, s1_in, cot_other_a, cot_other_b, *refs
):
    (
        gain_y, gain_m, w_qkv_hbm, w_out_hbm, w_up_hbm, w_down_hbm, sent,
        s1, cot, normed, qkv, mixed, s2, probs, acc, grad, grad_qkv,
        w_qkv, w_out, w_up, w_down, sems, late_sems,
    ) = refs[pieces:]
    cot_own = refs[:pieces]
    copies = fetch(sems, (w_qkv_hbm, w_qkv), (w_out_hbm, w_out))
    count, dim = s1.shape
    hidden = w_up.shape[1]
    part = length // pieces
    lines = count // length
    s1[...] = dot(one_hot(to_line[...]), s1_in[...]).astype(BF16)
    unit, _ = standardize(s1[...].astype(F32))
    normed[...] = (unit * gain_y[...]).astype(BF16)
    for i in range(lines):
        for k in range(pieces):
            if i < lines // 2:
                source, start = cot_own[k], i * part
            else:
                source = cot_other_a if k < pieces // 2 else cot_other_b
                start = (k % (pieces // 2) * (lines // 2) + i - lines // 2) * part
            cot[i * length + k * part : i * length + (k + 1) * part, :] = source[
                start : start + part, :
            ]
    copies[0].wait()
    late = fetch(late_sems, (w_up_hbm, w_up), (w_down_hbm, w_down))
    project_qkv(normed, w_qkv, qkv)
    blocks = Blocks(count, dim, length)
    attend(blocks, qkv, mixed, probs)
    copies[1].wait()
    low = (s1[...].astype(F32) + dot(mixed[...], w_out[...])).astype(BF16)
    s2[...] = low
    unit, _ = standardize(low.astype(F32))
    normed[...] = (unit * gain_m[...]).astype(BF16)

    for copy in late:
        copy.wait()
    chunk = 512 if hidden % 512 == 0 else hidden
    c0 = 0.7978845608028654
    c1 = 0.044715
    for c in range(hidden // chunk):
        cols = slice(c * chunk, (c + 1) * chunk)
        pre = dot(normed[...], w_up[:, cols])
        g_act = dot_t(cot[...], w_down[cols, :]).astype(BF16).astype(F32)
        square = pre * pre
        half = 0.5 * jnp.tanh(pre * (c0 + (c0 * c1) * square)) + 0.5
        slope = half + pre * (half - half * half) * (2 * c0 + (6 * c0 * c1) * square)
        g_pre = (g_act * slope).astype(BF16)
        part_sum = dot_t(g_pre, w_up[:, cols])
        acc[...] = part_sum if c == 0 else acc[...] + part_sum

    back = norm_back(s2[...].astype(F32), gain_m[...], acc[...])
    cot[...] = (cot[...].astype(F32) + back).astype(BF16)
    grad[...] = dot_t(cot[...], w_out[...]).astype(BF16)
    attend_back(blocks, qkv, grad, grad_qkv, probs)
    acc[...] = dot_t(grad_qkv[...], w_qkv[...])
    back = norm_back(s1[...].astype(F32), gain_y[...], acc[...])
    normed[...] = (cot[...].astype(F32) + back).astype(BF16)
    sent[...] = dot(one_hot(to_sent[...]), normed[...]).astype(BF16)


def x_back_body(shape, inputs, to_line, g1_in, qkv_hbm, gain, w_qkv_hbm, w_out_hbm, *refs):
    parts = refs[:inputs]
    *outs, whole, sent, g1, grad, grad_qkv, acc, qkv, w_qkv, w_out, sems = refs[inputs:]
    copies = fetch(
        sems,
        (w_out_hbm, w_out),
        (qkv_hbm, qkv),
        (w_qkv_hbm, w_qkv),
        *zip(parts, block_targets(whole, inputs)),
    )
    blocks, lines, part, dim = shape
    tok = whole.reshape(shape)
    target = sent if len(outs) > 1 else outs[0]
    sent_lines = target.reshape(shape)
    length = blocks * part
    g1[...] = dot(one_hot(to_line[...]), g1_in[...]).astype(BF16)
    copies[0].wait()
    grad[...] = dot_t(g1[...], w_out[...]).astype(BF16)
    copies[1].wait()
    attend_back(Blocks(g1.shape[0], dim, length), qkv, grad, grad_qkv)
    for copy in copies[2:]:
        copy.wait()
    acc[...] = dot_t(grad_qkv[...], w_qkv[...])
    for i in range(lines):
        rows = slice(i * length, (i + 1) * length)
        x = tok[:, i].reshape(length, dim).astype(F32)
        total = g1[rows, :].astype(F32) + norm_back(x, gain[...], acc[rows, :])
        sent_lines[:, i] = total.astype(BF16).reshape(blocks, part, dim)
    scatter_blocks(target, outs)


def call(body, name, outs, scratch, args, vmem_mib, in_hbm=(), flops=10**9):
    vmem = pl.BlockSpec(memory_space=pltpu.VMEM)
    return pl.pallas_call(
        body,
        out_shape=outs,
        in_specs=[
            pl.BlockSpec(memory_space=pl.ANY) if i in in_hbm else vmem for i in range(len(args))
        ],
        scratch_shapes=scratch,
        compiler_params=pltpu.CompilerParams(vmem_limit_bytes=vmem_mib * MIB),
        cost_estimate=pl.CostEstimate(flops=flops, bytes_accessed=4000000, transcendentals=0),
        name=name,
    )(*args)


def inverse(order):
    result = np.empty_like(order)
    result[order] = np.arange(order.size, dtype=order.dtype)
    return result


def row(order):
    return np.asarray(order, np.int32).reshape(1, -1)


def make_local(gh, gy):
    gx = NZ * gh

    def local(
        tokens, cotangent, gain_x, w_qkv_x, w_out_x, gain_y, w_qkv_y, w_out_y, gain_mlp, w_up,
        w_down,
    ):
        tx, ty, tz, dim = tokens.shape
        hidden = w_up.shape[1]
        count = tx * ty * tz
        y_lines = ty // gh
        own = tx // gy
        x_lines = tz * own
        len_x, len_y = tx * gx, ty * gy
        half, mine = lax.axis_index("gz"), lax.axis_index("gy")

        def vm(shape, dtype=BF16):
            return pltpu.VMEM(shape, dtype)

        def pick(options, index):
            table = jnp.asarray(np.stack([row(o) for o in options]))
            return lax.dynamic_index_in_dim(table, index, keepdims=False)

        tile_row = np.arange(count).reshape(tx, ty, tz)
        cot_orders = []
        for z in range(NZ):
            for g in range(gy):
                cut = tile_row.reshape(gy, own, ty, tz).transpose(0, 3, 1, 2)
                cut = cut[[g ^ k for k in range(gy)]][:, [z, 1 - z]]
                cot_orders.append(cut.reshape(-1))
        line_row = np.arange(count).reshape(y_lines, NZ, gh, gy, own)
        out_orders = [
            line_row[:, [z, 1 - z]].transpose(3, 2, 0, 1, 4).reshape(-1) for z in range(NZ)
        ]
        come_row = np.arange(count).reshape(gy, gh * y_lines, x_lines)
        y_orders = [
            come_row[[g ^ k for k in range(gy)]].transpose(2, 0, 1).reshape(-1)
            for g in range(gy)
        ]
        lane_blocks = dim // 128

        def packed(array):
            split = array.reshape(tx, ty, tz, lane_blocks, 128).transpose(0, 1, 3, 2, 4)
            return split.reshape(count * lane_blocks, 128)

        def exchange(parts, first):
            if len(parts) == 1:
                whole = parts[0].reshape(gx, count // gx, dim)
                moved = lax.all_to_all(whole, ("gz", "gh"), 0, 0, tiled=True)
                return [moved.reshape(count, dim)]
            moved = list(parts)
            for k in first:
                pairs = [(i, i ^ k) for i in range(gx)]
                moved[k] = lax.ppermute(parts[k], ("gz", "gh"), pairs)
            return moved

        flat = jax.ShapeDtypeStruct((count, dim), BF16)
        block = jax.ShapeDtypeStruct((count // gx, dim), BF16)
        far_first = [*range(gx // NZ, gx), *range(1, gx // NZ)]
        line_shape = (gx, y_lines, tx, dim)
        gain_x, gain_y, gain_mlp = (g.reshape(1, dim) for g in (gain_x, gain_y, gain_mlp))

        tok_sent = call(
            lambda *refs: unpack_tokens_body(tx, ty, tz, gh, *refs),
            "unpack_tokens",
            [flat],
            [vm((count, dim)), vm((count, dim))],
            (packed(tokens),),
            vmem_mib=10,
        )
        tok_x = exchange(tok_sent, far_first)

        cot_sent = call(
            lambda *refs: unpack_body(tz, *refs),
            "unpack_cotangent",
            flat,
            [vm((count, dim))],
            (pick([inverse(o) for o in cot_orders], half * gy + mine), packed(cotangent)),
            vmem_mib=10,
        ).reshape(gy, count // gy, dim)
        cot_own = [cot_sent[0]] + [
            lax.ppermute(cot_sent[k], "gy", [(i, i ^ k) for i in range(gy)])
            for k in range(1, gy)
        ]
        parts = [
            jnp.concatenate([piece[piece.shape[0] // 2 :] for piece in pieces], 0)
            for pieces in (cot_own[: gy // 2], cot_own[gy // 2 :])
        ]
        *parts, tok_x[0] = lax.optimization_barrier((*parts, tok_x[0]))
        cot_other = [lax.ppermute(part, "gz", [(0, 1), (1, 0)]) for part in parts]

        sent, qkv_x = call(
            lambda *refs: x_forward_body(line_shape, *refs),
            "x_forward",
            (flat, jax.ShapeDtypeStruct((count, 3 * dim), BF16)),
            [
                vm((count, dim)),
                vm((count, dim)),
                vm((count, dim)),
                vm((dim, 3 * dim)),
                vm((dim, dim)),
                pltpu.SemaphoreType.DMA((2,)),
            ],
            (pick([inverse(o) for o in out_orders], half), gain_x, w_qkv_x, w_out_x, *tok_x),
            vmem_mib=52,
            in_hbm=(2, 3),
            flops=3 * 10**9,
        )
        sent, cot_other[0] = lax.optimization_barrier((sent, cot_other[0]))
        s1_y = lax.all_to_all(
            sent.reshape(gh * gy, count // (gh * gy), dim), ("gy", "gh"), 0, 0, tiled=True
        ).reshape(count, dim)

        group = group_of(len_y)
        g1_sent = call(
            lambda *refs: middle_body(gy, len_y, *refs),
            "middle",
            flat,
            [
                vm((count, dim)),
                vm((count, dim)),
                vm((count, dim)),
                vm((count, 3 * dim)),
                vm((count, dim)),
                vm((count, dim)),
                vm((x_lines * HEADS // group, len_y, group * len_y), F32),
                vm((count, dim), F32),
                vm((count, dim)),
                vm((count, 3 * dim)),
                vm((dim, 3 * dim)),
                vm((dim, dim)),
                vm((dim, hidden)),
                vm((hidden, dim)),
                pltpu.SemaphoreType.DMA((2,)),
                pltpu.SemaphoreType.DMA((2,)),
            ],
            (
                pick([inverse(o) for o in y_orders], mine),
                pick(y_orders, mine),
                s1_y,
                *cot_other,
                *cot_own,
                gain_y, gain_mlp, w_qkv_y, w_out_y, w_up, w_down,
            ),
            vmem_mib=52,
            in_hbm=tuple(range(gy + 7, gy + 11)),
            flops=9 * 10**9,
        )
        g1_x = lax.all_to_all(
            g1_sent.reshape(gh * gy, count // (gh * gy), dim), ("gy", "gh"), 0, 0, tiled=True
        ).reshape(count, dim)

        gt_sent = call(
            lambda *refs: x_back_body(line_shape, len(tok_x), *refs),
            "x_back",
            [block] * gx,
            [
                vm((count, dim)),
                vm((count, dim)),
                vm((count, dim)),
                vm((count, dim)),
                vm((count, 3 * dim)),
                vm((count, dim), F32),
                vm((count, 3 * dim)),
                vm((dim, 3 * dim)),
                vm((dim, dim)),
                pltpu.SemaphoreType.DMA((3 + len(tok_x),)),
            ],
            (pick(out_orders, half), g1_x, qkv_x, gain_x, w_qkv_x, w_out_x, *tok_x),
            vmem_mib=52,
            in_hbm=(2, 4, 5, *range(6, 6 + len(tok_x))),
            flops=3 * 10**9,
        )
        gt = exchange(gt_sent, far_first)
        out = call(
            lambda *refs: pack_body(tx, ty, tz, gh, *refs),
            "pack",
            jax.ShapeDtypeStruct((count * lane_blocks, 128), BF16),
            [vm((count, dim)), vm((count, dim))],
            tuple(gt),
            vmem_mib=10,
        )
        split = out.reshape(tx, ty, lane_blocks, tz, 128).transpose(0, 1, 3, 2, 4)
        return split.reshape(tx, ty, tz, dim)

    return local


def solution(mesh):
    gx, gy = mesh.shape["gx"], mesh.shape["gy"]
    halved = Mesh(mesh.devices.reshape(NZ, gx // NZ, gy), ("gz", "gh", "gy"))
    tile = P(("gz", "gh"), "gy", None, None)
    return jax.shard_map(
        make_local(gx // NZ, gy),
        mesh=halved,
        in_specs=(tile, tile) + (P(),) * 9,
        out_specs=tile,
        check_vma=False,
    )
```

```python
import jax
import jax.numpy as jnp
import numpy as np
from jax import lax
from jax.experimental import pallas as pl
from jax.experimental.pallas import tpu as pltpu
from jax.sharding import Mesh
from jax.sharding import PartitionSpec as P

HEADS = 8
NZ = 2
EPS = 1e-05
F32 = jnp.float32
BF16 = jnp.bfloat16
MIB = 1024 * 1024


def dot(a, b):
    return jnp.dot(a, b, preferred_element_type=F32)


def dot_t(a, b):
    return lax.dot_general(a, b, (((1,), (1,)), ((), ())), preferred_element_type=F32)


def dot_lt(a, b):
    return lax.dot_general(a, b, (((0,), (0,)), ((), ())), preferred_element_type=F32)


def one_hot(target):
    size = target.shape[1]
    rows = lax.broadcasted_iota(jnp.int32, (size, size), 0)
    return jnp.where(rows == target, 1.0, 0.0).astype(BF16)


def digits(*sizes):
    count = 1
    for size in sizes:
        count *= size
    values = lax.broadcasted_iota(jnp.int32, (1, count), 1)
    found = []
    for size in reversed(sizes):
        if size & (size - 1) == 0:
            found.append(values & (size - 1))
            values = values >> (size.bit_length() - 1)
        else:
            found.append(lax.rem(values, size))
            values = lax.div(values, size)
    return found[::-1]


def gx_index(count):
    return lax.axis_index("gz") * (count // NZ) + lax.axis_index("gh")


def rows_at(start, size):
    return pl.ds(pl.multiple_of(start, size), size)


def standardize(x):
    centred = x - jnp.mean(x, -1, keepdims=True)
    inv = lax.rsqrt(jnp.mean(centred * centred, -1, keepdims=True) + EPS)
    return centred * inv, inv


def norm_back(x, gain, grad):
    unit, inv = standardize(x)
    scaled = grad * gain
    return inv * (
        scaled
        - jnp.mean(scaled, -1, keepdims=True)
        - unit * jnp.mean(scaled * unit, -1, keepdims=True)
    )


def group_of(length):
    return 4 if length * 4 <= 256 and HEADS % 4 == 0 else 2


def spread(block, count):
    width = block.shape[1] // count
    lane = lax.broadcasted_iota(jnp.int32, block.shape, 1)
    zero = jnp.zeros_like(block)
    return jnp.concatenate(
        [
            jnp.where((lane >= i * width) & (lane < (i + 1) * width), block, zero)
            for i in range(count)
        ],
        0,
    )


def gather(block, count):
    rows = block.shape[0] // count
    width = block.shape[1] // count
    lane = lax.broadcasted_iota(jnp.int32, (rows, block.shape[1]), 1)
    result = block[:rows]
    for i in range(1, count):
        result = jnp.where(lane >= i * width, block[i * rows : (i + 1) * rows], result)
    return result


class Blocks:
    def __init__(self, count, dim, length):
        self.group = group_of(length)
        self.dim = dim
        self.width = dim // HEADS * self.group
        self.scale = (dim // HEADS) ** -0.5
        self.items = [
            (slice(i * length, (i + 1) * length), j)
            for i in range(count // length)
            for j in range(HEADS // self.group)
        ]

    def lanes(self, j, part=0):
        return slice(part * self.dim + j * self.width, part * self.dim + (j + 1) * self.width)

    def q_wide(self, qkv, rows, j):
        return spread(qkv[rows, self.lanes(j)] * jnp.array(self.scale, BF16), self.group)


def softmax_rows(scores):
    exponent = jnp.exp(scores - jnp.max(scores, 0, keepdims=True))
    return exponent * (1.0 / jnp.sum(exponent, 0, keepdims=True))


def attend(blocks, qkv, mixed, keep=None):
    scores = [
        dot_t(qkv[rows, blocks.lanes(j, 1)], blocks.q_wide(qkv, rows, j))
        for rows, j in blocks.items
    ]
    lows = []
    for i, score in enumerate(scores):
        probs = softmax_rows(score)
        if keep is not None:
            keep[i] = probs
        lows.append(probs.astype(BF16))
    for (rows, j), low in zip(blocks.items, lows):
        out = dot_lt(low, qkv[rows, blocks.lanes(j, 2)])
        mixed[rows, blocks.lanes(j)] = gather(out, blocks.group).astype(BF16)


def attend_back(blocks, qkv, grad, grad_qkv, kept=None):
    probs_all, g_probs_all = [], []
    for rows, j in blocks.items:
        if kept is None:
            probs_all.append(dot_t(qkv[rows, blocks.lanes(j, 1)], blocks.q_wide(qkv, rows, j)))
        g_wide = spread(grad[rows, blocks.lanes(j)], blocks.group)
        g_probs_all.append(dot_t(qkv[rows, blocks.lanes(j, 2)], g_wide))
    lows, g_scores_all = [], []
    for i, g_probs in enumerate(g_probs_all):
        probs = softmax_rows(probs_all[i]) if kept is None else kept[i]
        weighted = probs * g_probs
        total = jnp.sum(weighted, 0, keepdims=True)
        g_scores_all.append((weighted - probs * total).astype(BF16))
        lows.append(probs.astype(BF16))
    for (rows, j), low, g_scores in zip(blocks.items, lows, g_scores_all):
        g_q = gather(dot_lt(g_scores, qkv[rows, blocks.lanes(j, 1)]), blocks.group)
        grad_qkv[rows, blocks.lanes(j)] = (g_q * blocks.scale).astype(BF16)
        g_k = dot(g_scores, blocks.q_wide(qkv, rows, j))
        grad_qkv[rows, blocks.lanes(j, 1)] = g_k.astype(BF16)
        g_v = dot(low, spread(grad[rows, blocks.lanes(j)], blocks.group))
        grad_qkv[rows, blocks.lanes(j, 2)] = g_v.astype(BF16)


def fetch(sems, *pairs):
    copies = [
        pltpu.make_async_copy(source, target, sems.at[i])
        for i, (source, target) in enumerate(pairs)
    ]
    for copy in copies:
        copy.start()
    return copies


def column_thirds(source, target):
    dim = source.shape[1] // 3
    cols = [pl.ds(j * dim, dim) for j in range(3)]
    return [(source.at[:, c], target.at[:, c]) for c in cols]


def project_qkv(normed, copies, w_qkv, qkv):
    dim = w_qkv.shape[0]
    for j in range(3):
        if j > 0:
            copies[j].wait()
        cols = slice(j * dim, (j + 1) * dim)
        qkv[:, cols] = dot(normed[...], w_qkv[:, cols]).astype(BF16)


def block_targets(whole, count):
    size = whole.shape[0] // count
    me = gx_index(count)
    return [whole.at[rows_at((me ^ k) * size, size)] for k in range(count)]


class Tile:
    def __init__(self, tx, ty, tz, dim):
        self.tx, self.ty, self.tz, self.blocks = tx, ty, tz, dim // 128
        self.run = 2 * self.blocks * tz

    def pick(self):
        x, y, c, z = digits(self.tx, 2, self.blocks, self.tz)
        return one_hot(((c * self.tz + z) * 2 + y) * self.tx + x)

    def packed_rows(self, j):
        starts = [(x * self.ty + 2 * j) * self.blocks * self.tz for x in range(self.tx)]
        return [slice(s, s + self.run) for s in starts]

    def places(self, j):
        return [
            (
                slice((z * self.ty + 2 * j + y) * self.tx, (z * self.ty + 2 * j + y + 1) * self.tx),
                slice(c * 128, (c + 1) * 128),
            )
            for c in range(self.blocks)
            for z in range(self.tz)
            for y in range(2)
        ]


def unpack_tokens_body(tile, packed, out):
    pick = tile.pick()
    for j in range(tile.ty // 2):
        slab = jnp.concatenate([packed[rows, :] for rows in tile.packed_rows(j)], 0)
        found = dot(pick, slab).astype(BF16)
        for i, (rows, lanes) in enumerate(tile.places(j)):
            out[rows, lanes] = found[i * tile.tx : (i + 1) * tile.tx]


def pack_body(tile, *refs):
    *parts, packed, whole = refs
    for part, target in zip(parts, block_targets(whole, len(parts))):
        target[...] = part[...]
    pick = tile.pick()
    for j in range(tile.ty // 2):
        slab = jnp.concatenate([whole[rows, lanes] for rows, lanes in tile.places(j)], 0)
        found = dot_lt(pick, slab).astype(BF16)
        for i, rows in enumerate(tile.packed_rows(j)):
            packed[rows, :] = found[i * tile.run : (i + 1) * tile.run]


def unpack_cotangent_body(tz, target, packed, out, rows):
    blocks = rows.shape[1] // 128
    step = 32 * tz
    slab = step * blocks
    place, block, z = digits(32, blocks, tz)
    pick = one_hot(block * step + place * tz + z)
    for s in range(packed.shape[0] // slab):
        found = dot(pick, packed[s * slab : (s + 1) * slab, :]).astype(BF16)
        for c in range(blocks):
            rows[s * step : (s + 1) * step, c * 128 : (c + 1) * 128] = found[
                c * step : (c + 1) * step
            ]
    out[...] = dot(one_hot(target[...]), rows[...]).astype(BF16)


class XLines:
    def __init__(self, lines, gh, gy, tx):
        self.lines, self.gh, self.gy, self.tx = lines, gh, gy, tx
        self.own = tx // gy
        self.chunk = lines * NZ * self.own
        self.small = self.chunk % 16 != 0 or tx % 16 != 0

    def pick_all(self):
        y, t, r, g, x = digits(self.lines, NZ, self.gh, self.gy, self.own)
        first = t ^ lax.axis_index("gz")
        return one_hot((((g * self.gh + r) * self.lines + y) * NZ + first) * self.own + x)

    def pick(self):
        y, t, g, x = digits(self.lines, NZ, self.gy, self.own)
        return one_hot(((g * self.lines + y) * NZ + t) * self.own + x)

    def line_runs(self, r):
        half = lax.axis_index("gz")
        return [
            rows_at(((y * NZ + (t ^ half)) * self.gh + r) * self.tx, self.tx)
            for y in range(self.lines)
            for t in range(NZ)
        ]

    def sent_runs(self, r):
        starts = [(g * self.gh + r) * self.chunk for g in range(self.gy)]
        return [slice(s, s + self.chunk) for s in starts]

    def send(self, source, sent):
        if self.small:
            sent[...] = dot(self.pick_all(), source[...]).astype(BF16)
            return
        pick = self.pick()
        for r in range(self.gh):
            block = jnp.concatenate([source[rows, :] for rows in self.line_runs(r)], 0)
            found = dot(pick, block).astype(BF16)
            for i, rows in enumerate(self.sent_runs(r)):
                sent[rows, :] = found[i * self.chunk : (i + 1) * self.chunk]

    def receive(self, sent, target):
        if self.small:
            target[...] = dot_lt(self.pick_all(), sent[...]).astype(BF16)
            return
        pick = self.pick()
        for r in range(self.gh):
            block = jnp.concatenate([sent[rows, :] for rows in self.sent_runs(r)], 0)
            found = dot_lt(pick, block).astype(BF16)
            for i, rows in enumerate(self.line_runs(r)):
                target[rows, :] = found[i * self.tx : (i + 1) * self.tx]


class YLines:
    def __init__(self, gy, ty, lines):
        self.gy, self.ty, self.lines = gy, ty, lines
        self.size = ty * lines

    def pick(self):
        y, x = digits(self.ty, self.lines)
        return one_hot(x * self.ty + y)

    def blocks(self):
        me = lax.axis_index("gy")
        for k in range(self.gy):
            starts = [(x * self.gy + k) * self.ty for x in range(self.lines)]
            runs = [slice(s, s + self.ty) for s in starts]
            yield rows_at((me ^ k) * self.size, self.size), runs

    def receive(self, sent, target):
        pick = self.pick()
        for rows, runs in self.blocks():
            found = dot(pick, sent[rows, :]).astype(BF16)
            for i, run in enumerate(runs):
                target[run, :] = found[i * self.ty : (i + 1) * self.ty]

    def send(self, source, sent):
        pick = self.pick()
        for rows, runs in self.blocks():
            block = jnp.concatenate([source[run, :] for run in runs], 0)
            sent[rows, :] = dot_lt(pick, block).astype(BF16)


def x_forward_body(
    shape, lines_x, gain, w_qkv_hbm, w_out_hbm, tok_flat, sent, qkv, normed, mixed, w_qkv, w_out,
    sems,
):
    copies = fetch(sems, *column_thirds(w_qkv_hbm, w_qkv), (w_out_hbm, w_out))
    tok = tok_flat.reshape(shape)
    blocks, lines, part, dim = shape
    length = blocks * part
    for i in range(lines):
        x = tok[:, i].reshape(length, dim).astype(F32)
        unit, _ = standardize(x)
        normed[i * length : (i + 1) * length, :] = (unit * gain[...]).astype(BF16)
    copies[0].wait()
    project_qkv(normed, copies, w_qkv, qkv)
    attend(Blocks(normed.shape[0], dim, length), qkv, mixed)
    copies[3].wait()
    out = dot(mixed[...], w_out[...])
    for i in range(lines):
        rows = slice(i * length, (i + 1) * length)
        x = tok[:, i].reshape(length, dim).astype(F32)
        normed[rows, :] = (x + out[rows]).astype(BF16)
    lines_x.send(normed, sent)


def grad_act_body(gather_rows, inputs, *refs):
    parts = refs[:inputs]
    w_down, cot, g_act = refs[inputs:]
    for rows, part, start in gather_rows:
        cot[rows, :] = parts[part][start : start + rows.stop - rows.start, :]
    g_act[...] = dot_t(cot[...], w_down[...]).astype(BF16)


def middle_body(
    lines_y, s1_in, cot_own, cot_other, g_own_hbm, g_other_hbm, gain_y, gain_m,
    w_qkv_hbm, w_out_hbm, w_up_hbm, sent,
    s1, cot, normed, qkv, mixed, s2, probs, acc, grad, grad_qkv, g_act, g_pre,
    w_qkv, w_out, w_up, sems, late_sems,
):
    copies = fetch(sems, *column_thirds(w_qkv_hbm, w_qkv), (w_out_hbm, w_out))
    count, dim = s1.shape
    hidden = w_up.shape[1]
    length = lines_y.gy * lines_y.ty
    half = count // 2
    lines_y.receive(s1_in, s1)
    unit, _ = standardize(s1[...].astype(F32))
    normed[...] = (unit * gain_y[...]).astype(BF16)
    copies[0].wait()
    late = fetch(
        late_sems,
        (w_up_hbm, w_up),
        (g_own_hbm, g_act.at[pl.ds(0, half)]),
        (g_other_hbm, g_act.at[pl.ds(half, half)]),
    )
    project_qkv(normed, copies, w_qkv, qkv)
    blocks = Blocks(count, dim, length)
    attend(blocks, qkv, mixed, probs)
    copies[3].wait()
    low = (s1[...].astype(F32) + dot(mixed[...], w_out[...])).astype(BF16)
    s2[...] = low
    unit, _ = standardize(low.astype(F32))
    normed[...] = (unit * gain_m[...]).astype(BF16)
    cot[:half, :] = cot_own[...]
    cot[half:, :] = cot_other[...]

    for copy in late:
        copy.wait()
    chunk = 256 if hidden % 256 == 0 else hidden
    c0 = 0.7978845608028654
    c1 = 0.044715
    for c in range(hidden // chunk):
        cols = slice(c * chunk, (c + 1) * chunk)
        pre = dot(normed[...], w_up[:, cols])
        square = pre * pre
        tanh = jnp.tanh(pre * (c0 + (c0 * c1) * square))
        twice = (1.0 + tanh) * (1.0 + (pre - pre * tanh) * (c0 + (3 * c0 * c1) * square))
        g_pre[:, cols] = ((0.5 * g_act[:, cols].astype(F32)) * twice).astype(BF16)
    acc[...] = dot_t(g_pre[...], w_up[...])

    back = norm_back(s2[...].astype(F32), gain_m[...], acc[...])
    cot[...] = (cot[...].astype(F32) + back).astype(BF16)
    grad[...] = dot_t(cot[...], w_out[...]).astype(BF16)
    attend_back(blocks, qkv, grad, grad_qkv, probs)
    acc[...] = dot_t(grad_qkv[...], w_qkv[...])
    back = norm_back(s1[...].astype(F32), gain_y[...], acc[...])
    normed[...] = (cot[...].astype(F32) + back).astype(BF16)
    lines_y.send(normed, sent)


def x_back_body(
    shape, lines_x, g1_in, qkv_hbm, gain, w_qkv_hbm, w_out_hbm, tok_hbm, *refs
):
    *outs, tok_flat, sent, g1, grad, grad_qkv, acc, qkv, w_qkv, w_out, sems, late_sems = refs
    copies = fetch(sems, (w_out_hbm, w_out), (qkv_hbm, qkv))
    blocks, lines, part, dim = shape
    length = blocks * part
    tok = tok_flat.reshape(shape)
    sent_lines = sent.reshape(shape)
    lines_x.receive(g1_in, g1)
    copies[0].wait()
    late = fetch(late_sems, (w_qkv_hbm, w_qkv), (tok_hbm, tok_flat))
    grad[...] = dot_t(g1[...], w_out[...]).astype(BF16)
    copies[1].wait()
    attend_back(Blocks(g1.shape[0], dim, length), qkv, grad, grad_qkv)
    for copy in late:
        copy.wait()
    acc[...] = dot_t(grad_qkv[...], w_qkv[...])
    for i in range(lines):
        rows = slice(i * length, (i + 1) * length)
        x = tok[:, i].reshape(length, dim).astype(F32)
        total = g1[rows, :].astype(F32) + norm_back(x, gain[...], acc[rows, :])
        sent_lines[:, i] = total.astype(BF16).reshape(blocks, part, dim)
    for source, out in zip(block_targets(sent, len(outs)), outs):
        out[...] = source[...]


def call(body, name, outs, scratch, args, vmem_mib, in_hbm=(), flops=10**9):
    vmem = pl.BlockSpec(memory_space=pltpu.VMEM)
    anywhere = pl.BlockSpec(memory_space=pl.ANY)
    return pl.pallas_call(
        body,
        out_shape=outs,
        in_specs=[anywhere if i in in_hbm else vmem for i in range(len(args))],
        scratch_shapes=scratch,
        compiler_params=pltpu.CompilerParams(vmem_limit_bytes=int(vmem_mib * MIB)),
        cost_estimate=pl.CostEstimate(flops=flops, bytes_accessed=4000000, transcendentals=0),
        name=name,
    )(*args)


def inverse(order):
    result = np.empty_like(order)
    result[order] = np.arange(order.size, dtype=order.dtype)
    return result


def make_local(gh, gy):
    gx = NZ * gh

    def local(
        tokens, cotangent, gain_x, w_qkv_x, w_out_x, gain_y, w_qkv_y, w_out_y, gain_mlp, w_up,
        w_down,
    ):
        tx, ty, tz, dim = tokens.shape
        hidden = w_up.shape[1]
        count = tx * ty * tz
        y_lines = ty // gh
        own = tx // gy
        x_lines = tz * own
        len_x, len_y = tx * gx, ty * gy
        line_shape = (gx, y_lines, tx, dim)
        tile = Tile(tx, ty, tz, dim)
        lines_x = XLines(y_lines, gh, gy, tx)
        lines_y = YLines(gy, ty, x_lines)
        flat = jax.ShapeDtypeStruct((count, dim), BF16)
        gain_x, gain_y, gain_mlp = (g.reshape(1, dim) for g in (gain_x, gain_y, gain_mlp))

        def vm(shape, dtype=BF16):
            return pltpu.VMEM(shape, dtype)

        def packed(array):
            split = array.reshape(tx, ty, tz, tile.blocks, 128).transpose(0, 1, 3, 2, 4)
            return split.reshape(count * tile.blocks, 128)

        def exchange(array, axes, parts):
            whole = array.reshape(parts, count // parts, dim)
            return lax.all_to_all(whole, axes, 0, 0, tiled=True).reshape(count, dim)

        tok_sent = call(
            lambda *refs: unpack_tokens_body(tile, *refs),
            "unpack_tokens",
            flat,
            [],
            (packed(tokens),),
            vmem_mib=10,
        )
        tok_x = exchange(tok_sent, ("gz", "gh"), gx)

        tile_row = np.arange(count).reshape(gy, own, ty, tz).transpose(0, 3, 1, 2)
        targets = []
        for z in range(NZ):
            for g in range(gy):
                order = tile_row[[g ^ k for k in range(gy)]][:, [z, 1 - z]].reshape(-1)
                targets.append(inverse(order).astype(np.int32).reshape(1, -1))
        target = lax.dynamic_index_in_dim(
            jnp.asarray(np.stack(targets)),
            lax.axis_index("gz") * gy + lax.axis_index("gy"),
            keepdims=False,
        )
        cot_sent = call(
            lambda *refs: unpack_cotangent_body(tz, *refs),
            "unpack_cotangent",
            flat,
            [vm((count, dim))],
            (target, packed(cotangent)),
            vmem_mib=10,
        ).reshape(gy, count // gy, dim)
        cot_own = [cot_sent[0]] + [
            lax.ppermute(cot_sent[k], "gy", [(i, i ^ k) for i in range(gy)])
            for k in range(1, gy)
        ]
        near = gy // 2
        parts = [
            jnp.concatenate([piece[piece.shape[0] // 2 :] for piece in pieces], 0)
            for pieces in (cot_own[:near], cot_own[near:])
        ]
        *parts, tok_x = lax.optimization_barrier((*parts, tok_x))
        cot_other = [lax.ppermute(part, "gz", [(0, 1), (1, 0)]) for part in parts]

        sent, qkv_x = call(
            lambda *refs: x_forward_body(line_shape, lines_x, *refs),
            "x_forward",
            (flat, jax.ShapeDtypeStruct((count, 3 * dim), BF16)),
            [
                vm((count, dim)),
                vm((count, dim)),
                vm((dim, 3 * dim)),
                vm((dim, dim)),
                pltpu.SemaphoreType.DMA((4,)),
            ],
            (gain_x, w_qkv_x, w_out_x, tok_x),
            vmem_mib=52,
            in_hbm=(1, 2),
            flops=3 * 10**9,
        )
        sent, cot_other[0] = lax.optimization_barrier((sent, cot_other[0]))
        s1_y = exchange(sent, ("gy", "gh"), gh * gy)

        def line_run(i, k):
            return slice((i * gy + k) * ty, (i * gy + k + 1) * ty)

        def grad_act(name, pieces, gather_rows):
            half = jax.ShapeDtypeStruct((count // 2, dim), BF16)
            return call(
                lambda *refs: grad_act_body(gather_rows, len(pieces), *refs),
                name,
                (half, jax.ShapeDtypeStruct((count // 2, hidden), BF16)),
                [],
                (*pieces, w_down),
                vmem_mib=16,
            )

        own_runs = [(line_run(i, k), k, i * ty) for i in range(own) for k in range(gy)]
        other_runs = [
            (line_run(i, k), k // near, (k % near * own + i) * ty)
            for i in range(own)
            for k in range(gy)
        ]
        cot_a, g_act_a = grad_act("grad_act_own", cot_own, own_runs)
        cot_b, g_act_b = grad_act("grad_act_other", cot_other, other_runs)

        group = group_of(len_y)
        g1_sent = call(
            lambda *refs: middle_body(lines_y, *refs),
            "middle",
            flat,
            [
                vm((count, dim)),
                vm((count, dim)),
                vm((count, dim)),
                vm((count, 3 * dim)),
                vm((count, dim)),
                vm((count, dim)),
                vm((x_lines * HEADS // group, len_y, group * len_y), F32),
                vm((count, dim), F32),
                vm((count, dim)),
                vm((count, 3 * dim)),
                vm((count, hidden)),
                vm((count, hidden)),
                vm((dim, 3 * dim)),
                vm((dim, dim)),
                vm((dim, hidden)),
                pltpu.SemaphoreType.DMA((4,)),
                pltpu.SemaphoreType.DMA((3,)),
            ],
            (
                s1_y, cot_a, cot_b, g_act_a, g_act_b, gain_y, gain_mlp,
                w_qkv_y, w_out_y, w_up,
            ),
            vmem_mib=52,
            in_hbm=(3, 4, 7, 8, 9),
            flops=9 * 10**9,
        )
        g1_x = exchange(g1_sent, ("gy", "gh"), gh * gy)

        gt_parts = call(
            lambda *refs: x_back_body(line_shape, lines_x, *refs),
            "x_back",
            [jax.ShapeDtypeStruct((count // gx, dim), BF16)] * gx,
            [
                vm((count, dim)),
                vm((count, dim)),
                vm((count, dim)),
                vm((count, dim)),
                vm((count, 3 * dim)),
                vm((count, dim), F32),
                vm((count, 3 * dim)),
                vm((dim, 3 * dim)),
                vm((dim, dim)),
                pltpu.SemaphoreType.DMA((2,)),
                pltpu.SemaphoreType.DMA((2,)),
            ],
            (g1_x, qkv_x, gain_x, w_qkv_x, w_out_x, tok_x),
            vmem_mib=52,
            in_hbm=(1, 3, 4, 5),
            flops=3 * 10**9,
        )
        gt = list(gt_parts)
        for k in [*range(gh, gx), *range(1, gh)]:
            gt[k] = lax.ppermute(gt[k], ("gz", "gh"), [(i, i ^ k) for i in range(gx)])
        out = call(
            lambda *refs: pack_body(tile, *refs),
            "pack",
            jax.ShapeDtypeStruct((count * tile.blocks, 128), BF16),
            [vm((count, dim))],
            tuple(gt),
            vmem_mib=10,
        )
        split = out.reshape(tx, ty, tile.blocks, tz, 128).transpose(0, 1, 3, 2, 4)
        return split.reshape(tx, ty, tz, dim)

    return local


def solution(mesh):
    gx, gy = mesh.shape["gx"], mesh.shape["gy"]
    halved = Mesh(mesh.devices.reshape(NZ, gx // NZ, gy), ("gz", "gh", "gy"))
    tile = P(("gz", "gh"), "gy", None, None)
    return jax.shard_map(
        make_local(gx // NZ, gy),
        mesh=halved,
        in_specs=(tile, tile) + (P(),) * 9,
        out_specs=tile,
        check_vma=False,
    )
```

```python
import jax
import jax.numpy as jnp
import numpy as np
from jax import lax
from jax.experimental import pallas as pl
from jax.experimental.pallas import tpu as pltpu
from jax.sharding import Mesh
from jax.sharding import PartitionSpec as P

HEADS = 8
GROUP = 2
NZ = 2
EPS = 1e-05
F32 = jnp.float32
BF16 = jnp.bfloat16
MIB = 1024 * 1024


def dot(a, b):
    return jnp.dot(a, b, preferred_element_type=F32)


def dot_t(a, b):
    return lax.dot_general(a, b, (((1,), (1,)), ((), ())), preferred_element_type=F32)


def dot_lt(a, b):
    return lax.dot_general(a, b, (((0,), (0,)), ((), ())), preferred_element_type=F32)


def one_hot(target):
    size = target.shape[1]
    rows = lax.broadcasted_iota(jnp.int32, (size, size), 0)
    return jnp.where(rows == target, 1.0, 0.0).astype(BF16)


def digits(*sizes):
    count = 1
    for size in sizes:
        count *= size
    values = lax.broadcasted_iota(jnp.int32, (1, count), 1)
    found = []
    for size in reversed(sizes):
        if size & (size - 1) == 0:
            found.append(values & (size - 1))
            values = values >> (size.bit_length() - 1)
        else:
            found.append(lax.rem(values, size))
            values = lax.div(values, size)
    return found[::-1]


def gx_index(count):
    return lax.axis_index("gz") * (count // NZ) + lax.axis_index("gh")


def rows_at(start, size):
    return pl.ds(pl.multiple_of(start, size), size)


def standardize(x):
    centred = x - jnp.mean(x, -1, keepdims=True)
    inv = lax.rsqrt(jnp.mean(centred * centred, -1, keepdims=True) + EPS)
    return centred * inv, inv


def norm_back(x, gain, grad):
    unit, inv = standardize(x)
    scaled = grad * gain
    return inv * (
        scaled
        - jnp.mean(scaled, -1, keepdims=True)
        - unit * jnp.mean(scaled * unit, -1, keepdims=True)
    )


def spread(block, count):
    width = block.shape[1] // count
    lane = lax.broadcasted_iota(jnp.int32, block.shape, 1)
    zero = jnp.zeros_like(block)
    return jnp.concatenate(
        [
            jnp.where((lane >= i * width) & (lane < (i + 1) * width), block, zero)
            for i in range(count)
        ],
        0,
    )


def gather(block, count):
    rows = block.shape[0] // count
    width = block.shape[1] // count
    lane = lax.broadcasted_iota(jnp.int32, (rows, block.shape[1]), 1)
    result = block[:rows]
    for i in range(1, count):
        result = jnp.where(lane >= i * width, block[i * rows : (i + 1) * rows], result)
    return result


class Blocks:
    def __init__(self, count, dim, length):
        self.group = GROUP
        self.dim = dim
        self.width = dim // HEADS * self.group
        self.scale = (dim // HEADS) ** -0.5
        self.items = [
            (slice(i * length, (i + 1) * length), j)
            for i in range(count // length)
            for j in range(HEADS // self.group)
        ]

    def lanes(self, j, part=0):
        return slice(part * self.dim + j * self.width, part * self.dim + (j + 1) * self.width)

    def q_wide(self, qkv, rows, j):
        return spread(qkv[rows, self.lanes(j)] * jnp.array(self.scale, BF16), self.group)


def softmax_rows(scores):
    exponent = jnp.exp(scores - jnp.max(scores, 0, keepdims=True))
    return exponent * (1.0 / jnp.sum(exponent, 0, keepdims=True))


def attend(blocks, qkv, mixed, keep=None):
    scores = [
        dot_t(qkv[rows, blocks.lanes(j, 1)], blocks.q_wide(qkv, rows, j))
        for rows, j in blocks.items
    ]
    lows = []
    for i, score in enumerate(scores):
        probs = softmax_rows(score)
        if keep is not None:
            keep[i] = probs
        lows.append(probs.astype(BF16))
    for (rows, j), low in zip(blocks.items, lows):
        out = dot_lt(low, qkv[rows, blocks.lanes(j, 2)])
        mixed[rows, blocks.lanes(j)] = gather(out, blocks.group).astype(BF16)


def attend_back(blocks, qkv, grad, grad_qkv, kept=None):
    probs_all, g_probs_all = [], []
    for rows, j in blocks.items:
        if kept is None:
            probs_all.append(dot_t(qkv[rows, blocks.lanes(j, 1)], blocks.q_wide(qkv, rows, j)))
        g_wide = spread(grad[rows, blocks.lanes(j)], blocks.group)
        g_probs_all.append(dot_t(qkv[rows, blocks.lanes(j, 2)], g_wide))
    lows, g_scores_all = [], []
    for i, g_probs in enumerate(g_probs_all):
        probs = softmax_rows(probs_all[i]) if kept is None else kept[i]
        weighted = probs * g_probs
        total = jnp.sum(weighted, 0, keepdims=True)
        g_scores_all.append((weighted - probs * total).astype(BF16))
        lows.append(probs.astype(BF16))
    for (rows, j), low, g_scores in zip(blocks.items, lows, g_scores_all):
        g_q = gather(dot_lt(g_scores, qkv[rows, blocks.lanes(j, 1)]), blocks.group)
        grad_qkv[rows, blocks.lanes(j)] = (g_q * blocks.scale).astype(BF16)
        g_k = dot(g_scores, blocks.q_wide(qkv, rows, j))
        grad_qkv[rows, blocks.lanes(j, 1)] = g_k.astype(BF16)
        g_v = dot(low, spread(grad[rows, blocks.lanes(j)], blocks.group))
        grad_qkv[rows, blocks.lanes(j, 2)] = g_v.astype(BF16)


def fetch(sems, *pairs):
    copies = [
        pltpu.make_async_copy(source, target, sems.at[i])
        for i, (source, target) in enumerate(pairs)
    ]
    for copy in copies:
        copy.start()
    return copies


def column_thirds(source, target):
    dim = source.shape[1] // 3
    cols = [pl.ds(j * dim, dim) for j in range(3)]
    return [(source.at[:, c], target.at[:, c]) for c in cols]


def project_qkv(normed, copies, w_qkv, qkv):
    dim = w_qkv.shape[0]
    for j in range(3):
        if j > 0:
            copies[j].wait()
        cols = slice(j * dim, (j + 1) * dim)
        qkv[:, cols] = dot(normed[...], w_qkv[:, cols]).astype(BF16)


def block_targets(whole, count):
    size = whole.shape[0] // count
    me = gx_index(count)
    return [whole.at[rows_at((me ^ k) * size, size)] for k in range(count)]


class Tile:
    def __init__(self, tx, ty, tz, dim):
        self.tx, self.ty, self.tz, self.blocks = tx, ty, tz, dim // 128
        self.run = 2 * self.blocks * tz

    def pick(self):
        x, y, c, z = digits(self.tx, 2, self.blocks, self.tz)
        return one_hot(((c * self.tz + z) * 2 + y) * self.tx + x)

    def packed_rows(self, j):
        starts = [(x * self.ty + 2 * j) * self.blocks * self.tz for x in range(self.tx)]
        return [slice(s, s + self.run) for s in starts]

    def places(self, j):
        return [
            (
                slice((z * self.ty + 2 * j + y) * self.tx, (z * self.ty + 2 * j + y + 1) * self.tx),
                slice(c * 128, (c + 1) * 128),
            )
            for c in range(self.blocks)
            for z in range(self.tz)
            for y in range(2)
        ]


def unpack_tokens_body(tile, packed, out):
    pick = tile.pick()
    for j in range(tile.ty // 2):
        slab = jnp.concatenate([packed[rows, :] for rows in tile.packed_rows(j)], 0)
        found = dot(pick, slab).astype(BF16)
        for i, (rows, lanes) in enumerate(tile.places(j)):
            out[rows, lanes] = found[i * tile.tx : (i + 1) * tile.tx]


def pack_body(tile, *refs):
    *parts, packed, whole = refs
    for part, target in zip(parts, block_targets(whole, len(parts))):
        target[...] = part[...]
    pick = tile.pick()
    for j in range(tile.ty // 2):
        slab = jnp.concatenate([whole[rows, lanes] for rows, lanes in tile.places(j)], 0)
        found = dot_lt(pick, slab).astype(BF16)
        for i, rows in enumerate(tile.packed_rows(j)):
            packed[rows, :] = found[i * tile.run : (i + 1) * tile.run]


def unpack_cotangent_body(tz, target, packed, out, rows):
    blocks = rows.shape[1] // 128
    step = 32 * tz
    slab = step * blocks
    place, block, z = digits(32, blocks, tz)
    pick = one_hot(block * step + place * tz + z)
    for s in range(packed.shape[0] // slab):
        found = dot(pick, packed[s * slab : (s + 1) * slab, :]).astype(BF16)
        for c in range(blocks):
            rows[s * step : (s + 1) * step, c * 128 : (c + 1) * 128] = found[
                c * step : (c + 1) * step
            ]
    out[...] = dot(one_hot(target[...]), rows[...]).astype(BF16)


class XLines:
    def __init__(self, lines, gh, gy, tx):
        self.lines, self.gh, self.gy, self.tx = lines, gh, gy, tx
        self.own = tx // gy
        self.chunk = lines * NZ * self.own
        self.small = self.chunk % 16 != 0 or tx % 16 != 0

    def pick_all(self):
        y, t, r, g, x = digits(self.lines, NZ, self.gh, self.gy, self.own)
        first = t ^ lax.axis_index("gz")
        return one_hot((((g * self.gh + r) * self.lines + y) * NZ + first) * self.own + x)

    def pick(self):
        y, t, g, x = digits(self.lines, NZ, self.gy, self.own)
        return one_hot(((g * self.lines + y) * NZ + t) * self.own + x)

    def line_runs(self, r):
        half = lax.axis_index("gz")
        return [
            rows_at(((y * NZ + (t ^ half)) * self.gh + r) * self.tx, self.tx)
            for y in range(self.lines)
            for t in range(NZ)
        ]

    def sent_runs(self, r):
        starts = [(g * self.gh + r) * self.chunk for g in range(self.gy)]
        return [slice(s, s + self.chunk) for s in starts]

    def send(self, source, sent):
        if self.small:
            sent[...] = dot(self.pick_all(), source[...]).astype(BF16)
            return
        pick = self.pick()
        for r in range(self.gh):
            block = jnp.concatenate([source[rows, :] for rows in self.line_runs(r)], 0)
            found = dot(pick, block).astype(BF16)
            for i, rows in enumerate(self.sent_runs(r)):
                sent[rows, :] = found[i * self.chunk : (i + 1) * self.chunk]

    def receive(self, sent, target):
        if self.small:
            target[...] = dot_lt(self.pick_all(), sent[...]).astype(BF16)
            return
        pick = self.pick()
        for r in range(self.gh):
            block = jnp.concatenate([sent[rows, :] for rows in self.sent_runs(r)], 0)
            found = dot_lt(pick, block).astype(BF16)
            for i, rows in enumerate(self.line_runs(r)):
                target[rows, :] = found[i * self.tx : (i + 1) * self.tx]


class YLines:
    def __init__(self, gy, ty, lines):
        self.gy, self.ty, self.lines = gy, ty, lines
        self.size = ty * lines

    def pick(self):
        y, x = digits(self.ty, self.lines)
        return one_hot(x * self.ty + y)

    def blocks(self):
        me = lax.axis_index("gy")
        for k in range(self.gy):
            starts = [(x * self.gy + k) * self.ty for x in range(self.lines)]
            runs = [slice(s, s + self.ty) for s in starts]
            yield rows_at((me ^ k) * self.size, self.size), runs

    def receive(self, sent, target):
        pick = self.pick()
        for rows, runs in self.blocks():
            found = dot(pick, sent[rows, :]).astype(BF16)
            for i, run in enumerate(runs):
                target[run, :] = found[i * self.ty : (i + 1) * self.ty]

    def send(self, source, sent):
        pick = self.pick()
        for rows, runs in self.blocks():
            block = jnp.concatenate([source[run, :] for run in runs], 0)
            sent[rows, :] = dot_lt(pick, block).astype(BF16)


def x_forward_body(
    shape, lines_x, gain, w_qkv_hbm, w_out_hbm, tok_flat, sent, qkv, normed, mixed, w_qkv, w_out,
    sems,
):
    copies = fetch(sems, *column_thirds(w_qkv_hbm, w_qkv), (w_out_hbm, w_out))
    tok = tok_flat.reshape(shape)
    blocks, lines, part, dim = shape
    length = blocks * part
    for i in range(lines):
        x = tok[:, i].reshape(length, dim).astype(F32)
        unit, _ = standardize(x)
        normed[i * length : (i + 1) * length, :] = (unit * gain[...]).astype(BF16)
    copies[0].wait()
    project_qkv(normed, copies, w_qkv, qkv)
    attend(Blocks(normed.shape[0], dim, length), qkv, mixed)
    copies[3].wait()
    out = dot(mixed[...], w_out[...])
    for i in range(lines):
        rows = slice(i * length, (i + 1) * length)
        x = tok[:, i].reshape(length, dim).astype(F32)
        normed[rows, :] = (x + out[rows]).astype(BF16)
    lines_x.send(normed, sent)


def grad_act_body(gather_rows, inputs, *refs):
    parts = refs[:inputs]
    w_down, cot, g_act = refs[inputs:]
    for rows, part, start in gather_rows:
        cot[rows, :] = parts[part][start : start + rows.stop - rows.start, :]
    g_act[...] = dot_t(cot[...], w_down[...]).astype(BF16)


def middle_body(
    lines_y, s1_in, cot_own, cot_other, g_own_hbm, g_other_hbm, gain_y, gain_m,
    w_qkv_hbm, w_out_hbm, w_up_hbm, sent,
    s1, cot, normed, qkv, mixed, s2, probs, acc, grad, grad_qkv, g_act, g_pre,
    w_qkv, w_out, w_up, sems, late_sems,
):
    copies = fetch(sems, *column_thirds(w_qkv_hbm, w_qkv), (w_out_hbm, w_out))
    count, dim = s1.shape
    hidden = w_up.shape[1]
    length = lines_y.gy * lines_y.ty
    half = count // 2
    lines_y.receive(s1_in, s1)
    unit, _ = standardize(s1[...].astype(F32))
    normed[...] = (unit * gain_y[...]).astype(BF16)
    copies[0].wait()
    late = fetch(
        late_sems,
        (w_up_hbm, w_up),
        (g_own_hbm, g_act.at[pl.ds(0, half)]),
        (g_other_hbm, g_act.at[pl.ds(half, half)]),
    )
    project_qkv(normed, copies, w_qkv, qkv)
    blocks = Blocks(count, dim, length)
    attend(blocks, qkv, mixed, probs)
    copies[3].wait()
    low = (s1[...].astype(F32) + dot(mixed[...], w_out[...])).astype(BF16)
    s2[...] = low
    unit, _ = standardize(low.astype(F32))
    normed[...] = (unit * gain_m[...]).astype(BF16)
    cot[:half, :] = cot_own[...]
    cot[half:, :] = cot_other[...]

    for copy in late:
        copy.wait()
    chunk = 256 if hidden % 256 == 0 else hidden
    c0 = 0.7978845608028654
    c1 = 0.044715
    for c in range(hidden // chunk):
        cols = slice(c * chunk, (c + 1) * chunk)
        pre = dot(normed[...], w_up[:, cols])
        square = pre * pre
        tanh = jnp.tanh(pre * (c0 + (c0 * c1) * square))
        twice = (1.0 + tanh) * (1.0 + (pre - pre * tanh) * (c0 + (3 * c0 * c1) * square))
        g_pre[:, cols] = ((0.5 * g_act[:, cols].astype(F32)) * twice).astype(BF16)
    acc[...] = dot_t(g_pre[...], w_up[...])

    back = norm_back(s2[...].astype(F32), gain_m[...], acc[...])
    cot[...] = (cot[...].astype(F32) + back).astype(BF16)
    grad[...] = dot_t(cot[...], w_out[...]).astype(BF16)
    attend_back(blocks, qkv, grad, grad_qkv, probs)
    acc[...] = dot_t(grad_qkv[...], w_qkv[...])
    back = norm_back(s1[...].astype(F32), gain_y[...], acc[...])
    normed[...] = (cot[...].astype(F32) + back).astype(BF16)
    lines_y.send(normed, sent)


def x_back_body(
    shape, lines_x, g1_in, qkv_hbm, gain, w_qkv_hbm, w_out_hbm, tok_hbm, *refs
):
    *outs, tok_flat, sent, g1, grad, grad_qkv, acc, qkv, w_qkv, w_out, sems, late_sems = refs
    copies = fetch(sems, (w_out_hbm, w_out), (qkv_hbm, qkv))
    blocks, lines, part, dim = shape
    length = blocks * part
    tok = tok_flat.reshape(shape)
    sent_lines = sent.reshape(shape)
    lines_x.receive(g1_in, g1)
    copies[0].wait()
    late = fetch(late_sems, (w_qkv_hbm, w_qkv), (tok_hbm, tok_flat))
    grad[...] = dot_t(g1[...], w_out[...]).astype(BF16)
    copies[1].wait()
    attend_back(Blocks(g1.shape[0], dim, length), qkv, grad, grad_qkv)
    for copy in late:
        copy.wait()
    acc[...] = dot_t(grad_qkv[...], w_qkv[...])
    for i in range(lines):
        rows = slice(i * length, (i + 1) * length)
        x = tok[:, i].reshape(length, dim).astype(F32)
        total = g1[rows, :].astype(F32) + norm_back(x, gain[...], acc[rows, :])
        sent_lines[:, i] = total.astype(BF16).reshape(blocks, part, dim)
    for source, out in zip(block_targets(sent, len(outs)), outs):
        out[...] = source[...]


def call(body, name, outs, scratch, args, vmem_mib, in_hbm=(), flops=10**9):
    vmem = pl.BlockSpec(memory_space=pltpu.VMEM)
    anywhere = pl.BlockSpec(memory_space=pl.ANY)
    return pl.pallas_call(
        body,
        out_shape=outs,
        in_specs=[anywhere if i in in_hbm else vmem for i in range(len(args))],
        scratch_shapes=scratch,
        compiler_params=pltpu.CompilerParams(vmem_limit_bytes=int(vmem_mib * MIB)),
        cost_estimate=pl.CostEstimate(flops=flops, bytes_accessed=4000000, transcendentals=0),
        name=name,
    )(*args)


def inverse(order):
    result = np.empty_like(order)
    result[order] = np.arange(order.size, dtype=order.dtype)
    return result


def make_local(gh, gy):
    gx = NZ * gh

    def local(
        tokens, cotangent, gain_x, w_qkv_x, w_out_x, gain_y, w_qkv_y, w_out_y, gain_mlp, w_up,
        w_down,
    ):
        tx, ty, tz, dim = tokens.shape
        hidden = w_up.shape[1]
        count = tx * ty * tz
        y_lines = ty // gh
        own = tx // gy
        x_lines = tz * own
        len_x, len_y = tx * gx, ty * gy
        line_shape = (gx, y_lines, tx, dim)
        tile = Tile(tx, ty, tz, dim)
        lines_x = XLines(y_lines, gh, gy, tx)
        lines_y = YLines(gy, ty, x_lines)
        flat = jax.ShapeDtypeStruct((count, dim), BF16)
        gain_x, gain_y, gain_mlp = (g.reshape(1, dim) for g in (gain_x, gain_y, gain_mlp))

        def vm(shape, dtype=BF16):
            return pltpu.VMEM(shape, dtype)

        def packed(array):
            split = array.reshape(tx, ty, tz, tile.blocks, 128).transpose(0, 1, 3, 2, 4)
            return split.reshape(count * tile.blocks, 128)

        def exchange(array, axes, parts):
            whole = array.reshape(parts, count // parts, dim)
            return lax.all_to_all(whole, axes, 0, 0, tiled=True).reshape(count, dim)

        tok_sent = call(
            lambda *refs: unpack_tokens_body(tile, *refs),
            "unpack_tokens",
            flat,
            [],
            (packed(tokens),),
            vmem_mib=10,
        )
        tok_x = exchange(tok_sent, ("gz", "gh"), gx)

        tile_row = np.arange(count).reshape(gy, own, ty, tz).transpose(0, 3, 1, 2)
        targets = []
        for z in range(NZ):
            for g in range(gy):
                order = tile_row[[g ^ k for k in range(gy)]][:, [z, 1 - z]].reshape(-1)
                targets.append(inverse(order).astype(np.int32).reshape(1, -1))
        target = lax.dynamic_index_in_dim(
            jnp.asarray(np.stack(targets)),
            lax.axis_index("gz") * gy + lax.axis_index("gy"),
            keepdims=False,
        )
        cot_sent = call(
            lambda *refs: unpack_cotangent_body(tz, *refs),
            "unpack_cotangent",
            flat,
            [vm((count, dim))],
            (target, packed(cotangent)),
            vmem_mib=10,
        ).reshape(gy, count // gy, dim)
        cot_own = [cot_sent[0]] + [
            lax.ppermute(cot_sent[k], "gy", [(i, i ^ k) for i in range(gy)])
            for k in range(1, gy)
        ]
        near = gy // 2
        parts = [
            jnp.concatenate([piece[piece.shape[0] // 2 :] for piece in pieces], 0)
            for pieces in (cot_own[:near], cot_own[near:])
        ]
        *parts, tok_x = lax.optimization_barrier((*parts, tok_x))
        cot_other = [lax.ppermute(part, "gz", [(0, 1), (1, 0)]) for part in parts]

        sent, qkv_x = call(
            lambda *refs: x_forward_body(line_shape, lines_x, *refs),
            "x_forward",
            (flat, jax.ShapeDtypeStruct((count, 3 * dim), BF16)),
            [
                vm((count, dim)),
                vm((count, dim)),
                vm((dim, 3 * dim)),
                vm((dim, dim)),
                pltpu.SemaphoreType.DMA((4,)),
            ],
            (gain_x, w_qkv_x, w_out_x, tok_x),
            vmem_mib=52,
            in_hbm=(1, 2),
            flops=3 * 10**9,
        )
        sent, cot_other[0] = lax.optimization_barrier((sent, cot_other[0]))
        s1_y = exchange(sent, ("gy", "gh"), gh * gy)

        def line_run(i, k):
            return slice((i * gy + k) * ty, (i * gy + k + 1) * ty)

        def grad_act(name, pieces, gather_rows):
            half = jax.ShapeDtypeStruct((count // 2, dim), BF16)
            return call(
                lambda *refs: grad_act_body(gather_rows, len(pieces), *refs),
                name,
                (half, jax.ShapeDtypeStruct((count // 2, hidden), BF16)),
                [],
                (*pieces, w_down),
                vmem_mib=16,
            )

        own_runs = [(line_run(i, k), k, i * ty) for i in range(own) for k in range(gy)]
        other_runs = [
            (line_run(i, k), k // near, (k % near * own + i) * ty)
            for i in range(own)
            for k in range(gy)
        ]
        cot_a, g_act_a = grad_act("grad_act_own", cot_own, own_runs)
        cot_b, g_act_b = grad_act("grad_act_other", cot_other, other_runs)

        g1_sent = call(
            lambda *refs: middle_body(lines_y, *refs),
            "middle",
            flat,
            [
                vm((count, dim)),
                vm((count, dim)),
                vm((count, dim)),
                vm((count, 3 * dim)),
                vm((count, dim)),
                vm((count, dim)),
                vm((x_lines * HEADS // GROUP, len_y, GROUP * len_y), F32),
                vm((count, dim), F32),
                vm((count, dim)),
                vm((count, 3 * dim)),
                vm((count, hidden)),
                vm((count, hidden)),
                vm((dim, 3 * dim)),
                vm((dim, dim)),
                vm((dim, hidden)),
                pltpu.SemaphoreType.DMA((4,)),
                pltpu.SemaphoreType.DMA((3,)),
            ],
            (
                s1_y, cot_a, cot_b, g_act_a, g_act_b, gain_y, gain_mlp,
                w_qkv_y, w_out_y, w_up,
            ),
            vmem_mib=52,
            in_hbm=(3, 4, 7, 8, 9),
            flops=9 * 10**9,
        )
        g1_x = exchange(g1_sent, ("gy", "gh"), gh * gy)

        gt_parts = call(
            lambda *refs: x_back_body(line_shape, lines_x, *refs),
            "x_back",
            [jax.ShapeDtypeStruct((count // gx, dim), BF16)] * gx,
            [
                vm((count, dim)),
                vm((count, dim)),
                vm((count, dim)),
                vm((count, dim)),
                vm((count, 3 * dim)),
                vm((count, dim), F32),
                vm((count, 3 * dim)),
                vm((dim, 3 * dim)),
                vm((dim, dim)),
                pltpu.SemaphoreType.DMA((2,)),
                pltpu.SemaphoreType.DMA((2,)),
            ],
            (g1_x, qkv_x, gain_x, w_qkv_x, w_out_x, tok_x),
            vmem_mib=52,
            in_hbm=(1, 3, 4, 5),
            flops=3 * 10**9,
        )
        gt = list(gt_parts)
        for k in [*range(gh, gx), *range(1, gh)]:
            gt[k] = lax.ppermute(gt[k], ("gz", "gh"), [(i, i ^ k) for i in range(gx)])
        out = call(
            lambda *refs: pack_body(tile, *refs),
            "pack",
            jax.ShapeDtypeStruct((count * tile.blocks, 128), BF16),
            [vm((count, dim))],
            tuple(gt),
            vmem_mib=10,
        )
        split = out.reshape(tx, ty, tile.blocks, tz, 128).transpose(0, 1, 3, 2, 4)
        return split.reshape(tx, ty, tz, dim)

    return local


def solution(mesh):
    gx, gy = mesh.shape["gx"], mesh.shape["gy"]
    halved = Mesh(mesh.devices.reshape(NZ, gx // NZ, gy), ("gz", "gh", "gy"))
    tile = P(("gz", "gh"), "gy", None, None)
    return jax.shard_map(
        make_local(gx // NZ, gy),
        mesh=halved,
        in_specs=(tile, tile) + (P(),) * 9,
        out_specs=tile,
        check_vma=False,
    )
```

```python
import jax
import jax.numpy as jnp
import numpy as np
from jax import lax
from jax.experimental import pallas as pl
from jax.experimental.pallas import tpu as pltpu
from jax.sharding import Mesh
from jax.sharding import PartitionSpec as P

HEADS = 8
GROUP = 2
NZ = 2
EPS = 1e-05
F32 = jnp.float32
BF16 = jnp.bfloat16
MIB = 1024 * 1024


def dot(a, b):
    return jnp.dot(a, b, preferred_element_type=F32)


def dot_t(a, b):
    return lax.dot_general(a, b, (((1,), (1,)), ((), ())), preferred_element_type=F32)


def dot_lt(a, b):
    return lax.dot_general(a, b, (((0,), (0,)), ((), ())), preferred_element_type=F32)


def one_hot(target):
    size = target.shape[1]
    rows = lax.broadcasted_iota(jnp.int32, (size, size), 0)
    return jnp.where(rows == target, 1.0, 0.0).astype(BF16)


def digits(*sizes):
    count = 1
    for size in sizes:
        count *= size
    values = lax.broadcasted_iota(jnp.int32, (1, count), 1)
    found = []
    for size in reversed(sizes):
        if size & (size - 1) == 0:
            found.append(values & (size - 1))
            values = values >> (size.bit_length() - 1)
        else:
            found.append(lax.rem(values, size))
            values = lax.div(values, size)
    return found[::-1]


def gx_index(count):
    return lax.axis_index("gz") * (count // NZ) + lax.axis_index("gh")


def rows_at(start, size):
    return pl.ds(pl.multiple_of(start, size), size)


def standardize(x):
    centred = x - jnp.mean(x, -1, keepdims=True)
    inv = lax.rsqrt(jnp.mean(centred * centred, -1, keepdims=True) + EPS)
    return centred * inv, inv


def norm_back(x, gain, grad):
    unit, inv = standardize(x)
    scaled = grad * gain
    return inv * (
        scaled
        - jnp.mean(scaled, -1, keepdims=True)
        - unit * jnp.mean(scaled * unit, -1, keepdims=True)
    )


def spread(block, count):
    width = block.shape[1] // count
    lane = lax.broadcasted_iota(jnp.int32, block.shape, 1)
    zero = jnp.zeros_like(block)
    return jnp.concatenate(
        [
            jnp.where((lane >= i * width) & (lane < (i + 1) * width), block, zero)
            for i in range(count)
        ],
        0,
    )


def gather(block, count):
    rows = block.shape[0] // count
    width = block.shape[1] // count
    lane = lax.broadcasted_iota(jnp.int32, (rows, block.shape[1]), 1)
    result = block[:rows]
    for i in range(1, count):
        result = jnp.where(lane >= i * width, block[i * rows : (i + 1) * rows], result)
    return result


class Blocks:
    def __init__(self, count, dim, length):
        self.group = GROUP
        self.dim = dim
        self.width = dim // HEADS * self.group
        self.scale = (dim // HEADS) ** -0.5
        self.items = [
            (slice(i * length, (i + 1) * length), j)
            for i in range(count // length)
            for j in range(HEADS // self.group)
        ]

    def lanes(self, j, part=0):
        return slice(part * self.dim + j * self.width, part * self.dim + (j + 1) * self.width)

    def q_wide(self, qkv, rows, j):
        return spread(qkv[rows, self.lanes(j)] * jnp.array(self.scale, BF16), self.group)


def softmax_rows(scores):
    exponent = jnp.exp(scores - jnp.max(scores, 0, keepdims=True))
    return exponent * (1.0 / jnp.sum(exponent, 0, keepdims=True))


def attend(blocks, qkv, mixed, keep=None):
    scores = [
        dot_t(qkv[rows, blocks.lanes(j, 1)], blocks.q_wide(qkv, rows, j))
        for rows, j in blocks.items
    ]
    lows = []
    for i, score in enumerate(scores):
        probs = softmax_rows(score)
        if keep is not None:
            keep[i] = probs
        lows.append(probs.astype(BF16))
    for (rows, j), low in zip(blocks.items, lows):
        out = dot_lt(low, qkv[rows, blocks.lanes(j, 2)])
        mixed[rows, blocks.lanes(j)] = gather(out, blocks.group).astype(BF16)


def attend_back(blocks, qkv, grad, grad_qkv, kept=None):
    probs_all, g_probs_all, q_wides, g_wides = [], [], [], []
    for rows, j in blocks.items:
        q_wide = blocks.q_wide(qkv, rows, j)
        if kept is None:
            probs_all.append(dot_t(qkv[rows, blocks.lanes(j, 1)], q_wide))
        g_wide = spread(grad[rows, blocks.lanes(j)], blocks.group)
        q_wides.append(q_wide)
        g_wides.append(g_wide)
        g_probs_all.append(dot_t(qkv[rows, blocks.lanes(j, 2)], g_wide))
    lows, g_scores_all = [], []
    for i, g_probs in enumerate(g_probs_all):
        probs = softmax_rows(probs_all[i]) if kept is None else kept[i]
        weighted = probs * g_probs
        total = jnp.sum(weighted, 0, keepdims=True)
        g_scores_all.append((weighted - probs * total).astype(BF16))
        lows.append(probs.astype(BF16))
    for (rows, j), low, g_scores, q_wide, g_wide in zip(
        blocks.items, lows, g_scores_all, q_wides, g_wides
    ):
        g_q = gather(dot_lt(g_scores, qkv[rows, blocks.lanes(j, 1)]), blocks.group)
        grad_qkv[rows, blocks.lanes(j)] = (g_q * blocks.scale).astype(BF16)
        g_k = dot(g_scores, q_wide)
        grad_qkv[rows, blocks.lanes(j, 1)] = g_k.astype(BF16)
        g_v = dot(low, g_wide)
        grad_qkv[rows, blocks.lanes(j, 2)] = g_v.astype(BF16)


def fetch(sems, *pairs):
    copies = [
        pltpu.make_async_copy(source, target, sems.at[i])
        for i, (source, target) in enumerate(pairs)
    ]
    for copy in copies:
        copy.start()
    return copies


def column_thirds(source, target):
    dim = source.shape[1] // 3
    cols = [pl.ds(j * dim, dim) for j in range(3)]
    return [(source.at[:, c], target.at[:, c]) for c in cols]


def project_qkv(normed, copies, w_qkv, qkv):
    dim = w_qkv.shape[0]
    for j in range(3):
        if j > 0:
            copies[j].wait()
        cols = slice(j * dim, (j + 1) * dim)
        qkv[:, cols] = dot(normed[...], w_qkv[:, cols]).astype(BF16)


def block_targets(whole, count):
    size = whole.shape[0] // count
    me = gx_index(count)
    return [whole.at[rows_at((me ^ k) * size, size)] for k in range(count)]


class Tile:
    def __init__(self, tx, ty, tz, dim):
        self.tx, self.ty, self.tz, self.blocks = tx, ty, tz, dim // 128
        self.run = 2 * self.blocks * tz

    def pick(self):
        x, y, c, z = digits(self.tx, 2, self.blocks, self.tz)
        return one_hot(((c * self.tz + z) * 2 + y) * self.tx + x)

    def packed_rows(self, j):
        starts = [(x * self.ty + 2 * j) * self.blocks * self.tz for x in range(self.tx)]
        return [slice(s, s + self.run) for s in starts]

    def places(self, j):
        return [
            (
                slice((z * self.ty + 2 * j + y) * self.tx, (z * self.ty + 2 * j + y + 1) * self.tx),
                slice(c * 128, (c + 1) * 128),
            )
            for c in range(self.blocks)
            for z in range(self.tz)
            for y in range(2)
        ]


def unpack_tokens_body(tile, packed, out):
    pick = tile.pick()
    for j in range(tile.ty // 2):
        slab = jnp.concatenate([packed[rows, :] for rows in tile.packed_rows(j)], 0)
        found = dot(pick, slab).astype(BF16)
        for i, (rows, lanes) in enumerate(tile.places(j)):
            out[rows, lanes] = found[i * tile.tx : (i + 1) * tile.tx]


def pack_body(tile, *refs):
    *parts, packed, whole = refs
    for part, target in zip(parts, block_targets(whole, len(parts))):
        target[...] = part[...]
    pick = tile.pick()
    for j in range(tile.ty // 2):
        slab = jnp.concatenate([whole[rows, lanes] for rows, lanes in tile.places(j)], 0)
        found = dot_lt(pick, slab).astype(BF16)
        for i, rows in enumerate(tile.packed_rows(j)):
            packed[rows, :] = found[i * tile.run : (i + 1) * tile.run]


def unpack_cotangent_body(tz, target, packed, out, rows):
    blocks = rows.shape[1] // 128
    step = 32 * tz
    slab = step * blocks
    place, block, z = digits(32, blocks, tz)
    pick = one_hot(block * step + place * tz + z)
    for s in range(packed.shape[0] // slab):
        found = dot(pick, packed[s * slab : (s + 1) * slab, :]).astype(BF16)
        for c in range(blocks):
            rows[s * step : (s + 1) * step, c * 128 : (c + 1) * 128] = found[
                c * step : (c + 1) * step
            ]
    out[...] = dot(one_hot(target[...]), rows[...]).astype(BF16)


class XLines:
    def __init__(self, lines, gh, gy, tx):
        self.lines, self.gh, self.gy, self.tx = lines, gh, gy, tx
        self.own = tx // gy
        self.chunk = lines * NZ * self.own
        self.small = self.chunk % 16 != 0 or tx % 16 != 0

    def pick_all(self):
        y, t, r, g, x = digits(self.lines, NZ, self.gh, self.gy, self.own)
        first = t ^ lax.axis_index("gz")
        return one_hot((((g * self.gh + r) * self.lines + y) * NZ + first) * self.own + x)

    def pick(self):
        y, t, g, x = digits(self.lines, NZ, self.gy, self.own)
        return one_hot(((g * self.lines + y) * NZ + t) * self.own + x)

    def line_runs(self, r):
        half = lax.axis_index("gz")
        return [
            rows_at(((y * NZ + (t ^ half)) * self.gh + r) * self.tx, self.tx)
            for y in range(self.lines)
            for t in range(NZ)
        ]

    def sent_runs(self, r):
        starts = [(g * self.gh + r) * self.chunk for g in range(self.gy)]
        return [slice(s, s + self.chunk) for s in starts]

    def send(self, source, sent):
        if self.small:
            sent[...] = dot(self.pick_all(), source[...]).astype(BF16)
            return
        pick = self.pick()
        for r in range(self.gh):
            block = jnp.concatenate([source[rows, :] for rows in self.line_runs(r)], 0)
            found = dot(pick, block).astype(BF16)
            for i, rows in enumerate(self.sent_runs(r)):
                sent[rows, :] = found[i * self.chunk : (i + 1) * self.chunk]

    def receive(self, sent, target):
        if self.small:
            target[...] = dot_lt(self.pick_all(), sent[...]).astype(BF16)
            return
        pick = self.pick()
        for r in range(self.gh):
            block = jnp.concatenate([sent[rows, :] for rows in self.sent_runs(r)], 0)
            found = dot_lt(pick, block).astype(BF16)
            for i, rows in enumerate(self.line_runs(r)):
                target[rows, :] = found[i * self.tx : (i + 1) * self.tx]


class YLines:
    def __init__(self, gy, ty, lines):
        self.gy, self.ty, self.lines = gy, ty, lines
        self.size = ty * lines

    def pick(self):
        y, x = digits(self.ty, self.lines)
        return one_hot(x * self.ty + y)

    def blocks(self):
        me = lax.axis_index("gy")
        for k in range(self.gy):
            starts = [(x * self.gy + k) * self.ty for x in range(self.lines)]
            runs = [slice(s, s + self.ty) for s in starts]
            yield rows_at((me ^ k) * self.size, self.size), runs

    def receive(self, sent, target):
        pick = self.pick()
        for rows, runs in self.blocks():
            found = dot(pick, sent[rows, :]).astype(BF16)
            for i, run in enumerate(runs):
                target[run, :] = found[i * self.ty : (i + 1) * self.ty]

    def send(self, source, sent):
        pick = self.pick()
        for rows, runs in self.blocks():
            block = jnp.concatenate([source[run, :] for run in runs], 0)
            sent[rows, :] = dot_lt(pick, block).astype(BF16)


def x_forward_body(
    shape, lines_x, gain, w_qkv_hbm, w_out_hbm, tok_flat, sent, qkv, normed, mixed, w_qkv, w_out,
    sems,
):
    copies = fetch(sems, *column_thirds(w_qkv_hbm, w_qkv), (w_out_hbm, w_out))
    tok = tok_flat.reshape(shape)
    blocks, lines, part, dim = shape
    length = blocks * part
    for i in range(lines):
        x = tok[:, i].reshape(length, dim).astype(F32)
        unit, _ = standardize(x)
        normed[i * length : (i + 1) * length, :] = (unit * gain[...]).astype(BF16)
    copies[0].wait()
    project_qkv(normed, copies, w_qkv, qkv)
    attend(Blocks(normed.shape[0], dim, length), qkv, mixed)
    copies[3].wait()
    out = dot(mixed[...], w_out[...])
    for i in range(lines):
        rows = slice(i * length, (i + 1) * length)
        x = tok[:, i].reshape(length, dim).astype(F32)
        normed[rows, :] = (x + out[rows]).astype(BF16)
    lines_x.send(normed, sent)


def grad_act_body(gather_rows, inputs, *refs):
    parts = refs[:inputs]
    w_down, cot, g_act = refs[inputs:]
    for rows, part, start in gather_rows:
        cot[rows, :] = parts[part][start : start + rows.stop - rows.start, :]
    g_act[...] = dot_t(cot[...], w_down[...]).astype(BF16)


def middle_body(
    lines_y, s1_in, cot_own, cot_other, g_own_hbm, g_other_hbm, gain_y, gain_m,
    w_qkv_hbm, w_out_hbm, w_up_hbm, sent,
    s1, cot, normed, qkv, mixed, s2, probs, acc, grad, grad_qkv, g_act, g_pre,
    w_qkv, w_out, w_up, sems, late_sems,
):
    copies = fetch(sems, *column_thirds(w_qkv_hbm, w_qkv), (w_out_hbm, w_out))
    count, dim = s1.shape
    hidden = w_up.shape[1]
    length = lines_y.gy * lines_y.ty
    half = count // 2
    lines_y.receive(s1_in, s1)
    unit, _ = standardize(s1[...].astype(F32))
    normed[...] = (unit * gain_y[...]).astype(BF16)
    copies[0].wait()
    late = fetch(
        late_sems,
        (w_up_hbm, w_up),
        (g_own_hbm, g_act.at[pl.ds(0, half)]),
        (g_other_hbm, g_act.at[pl.ds(half, half)]),
    )
    project_qkv(normed, copies, w_qkv, qkv)
    blocks = Blocks(count, dim, length)
    attend(blocks, qkv, mixed, probs)
    copies[3].wait()
    low = (s1[...].astype(F32) + dot(mixed[...], w_out[...])).astype(BF16)
    s2[...] = low
    unit, _ = standardize(low.astype(F32))
    normed[...] = (unit * gain_m[...]).astype(BF16)
    cot[:half, :] = cot_own[...]
    cot[half:, :] = cot_other[...]

    for copy in late:
        copy.wait()
    chunk = 256 if hidden % 256 == 0 else hidden
    c0 = 0.7978845608028654
    c1 = 0.044715
    for c in range(hidden // chunk):
        cols = slice(c * chunk, (c + 1) * chunk)
        pre = dot(normed[...], w_up[:, cols])
        square = pre * pre
        tanh = jnp.tanh(pre * (c0 + (c0 * c1) * square))
        twice = (1.0 + tanh) * (1.0 + (pre - pre * tanh) * (c0 + (3 * c0 * c1) * square))
        g_pre[:, cols] = ((0.5 * g_act[:, cols].astype(F32)) * twice).astype(BF16)
    acc[...] = dot_t(g_pre[...], w_up[...])

    back = norm_back(s2[...].astype(F32), gain_m[...], acc[...])
    cot[...] = (cot[...].astype(F32) + back).astype(BF16)
    grad[...] = dot_t(cot[...], w_out[...]).astype(BF16)
    attend_back(blocks, qkv, grad, grad_qkv, probs)
    acc[...] = dot_t(grad_qkv[...], w_qkv[...])
    back = norm_back(s1[...].astype(F32), gain_y[...], acc[...])
    normed[...] = (cot[...].astype(F32) + back).astype(BF16)
    lines_y.send(normed, sent)


def x_back_body(
    shape, lines_x, g1_in, qkv_hbm, gain, w_qkv_hbm, w_out_hbm, tok_hbm, *refs
):
    *outs, tok_flat, sent, g1, grad, grad_qkv, acc, qkv, w_qkv, w_out, sems, late_sems = refs
    copies = fetch(sems, (w_out_hbm, w_out), (qkv_hbm, qkv))
    blocks, lines, part, dim = shape
    length = blocks * part
    tok = tok_flat.reshape(shape)
    sent_lines = sent.reshape(shape)
    lines_x.receive(g1_in, g1)
    copies[0].wait()
    late = fetch(late_sems, (w_qkv_hbm, w_qkv), (tok_hbm, tok_flat))
    grad[...] = dot_t(g1[...], w_out[...]).astype(BF16)
    copies[1].wait()
    attend_back(Blocks(g1.shape[0], dim, length), qkv, grad, grad_qkv)
    for copy in late:
        copy.wait()
    acc[...] = dot_t(grad_qkv[...], w_qkv[...])
    for i in range(lines):
        rows = slice(i * length, (i + 1) * length)
        x = tok[:, i].reshape(length, dim).astype(F32)
        total = g1[rows, :].astype(F32) + norm_back(x, gain[...], acc[rows, :])
        sent_lines[:, i] = total.astype(BF16).reshape(blocks, part, dim)
    for source, out in zip(block_targets(sent, len(outs)), outs):
        out[...] = source[...]


def call(body, name, outs, scratch, args, vmem_mib, in_hbm=(), flops=10**9):
    vmem = pl.BlockSpec(memory_space=pltpu.VMEM)
    anywhere = pl.BlockSpec(memory_space=pl.ANY)
    return pl.pallas_call(
        body,
        out_shape=outs,
        in_specs=[anywhere if i in in_hbm else vmem for i in range(len(args))],
        scratch_shapes=scratch,
        compiler_params=pltpu.CompilerParams(vmem_limit_bytes=int(vmem_mib * MIB)),
        cost_estimate=pl.CostEstimate(flops=flops, bytes_accessed=4000000, transcendentals=0),
        name=name,
    )(*args)


def inverse(order):
    result = np.empty_like(order)
    result[order] = np.arange(order.size, dtype=order.dtype)
    return result


def make_local(gh, gy):
    gx = NZ * gh

    def local(
        tokens, cotangent, gain_x, w_qkv_x, w_out_x, gain_y, w_qkv_y, w_out_y, gain_mlp, w_up,
        w_down,
    ):
        tx, ty, tz, dim = tokens.shape
        hidden = w_up.shape[1]
        count = tx * ty * tz
        y_lines = ty // gh
        own = tx // gy
        x_lines = tz * own
        len_x, len_y = tx * gx, ty * gy
        line_shape = (gx, y_lines, tx, dim)
        tile = Tile(tx, ty, tz, dim)
        lines_x = XLines(y_lines, gh, gy, tx)
        lines_y = YLines(gy, ty, x_lines)
        flat = jax.ShapeDtypeStruct((count, dim), BF16)
        gain_x, gain_y, gain_mlp = (g.reshape(1, dim) for g in (gain_x, gain_y, gain_mlp))

        def vm(shape, dtype=BF16):
            return pltpu.VMEM(shape, dtype)

        def packed(array):
            split = array.reshape(tx, ty, tz, tile.blocks, 128).transpose(0, 1, 3, 2, 4)
            return split.reshape(count * tile.blocks, 128)

        def exchange(array, axes, parts):
            whole = array.reshape(parts, count // parts, dim)
            return lax.all_to_all(whole, axes, 0, 0, tiled=True).reshape(count, dim)

        tok_sent = call(
            lambda *refs: unpack_tokens_body(tile, *refs),
            "unpack_tokens",
            flat,
            [],
            (packed(tokens),),
            vmem_mib=10,
        )
        tok_x = exchange(tok_sent, ("gz", "gh"), gx)

        tile_row = np.arange(count).reshape(gy, own, ty, tz).transpose(0, 3, 1, 2)
        targets = []
        for z in range(NZ):
            for g in range(gy):
                order = tile_row[[g ^ k for k in range(gy)]][:, [z, 1 - z]].reshape(-1)
                targets.append(inverse(order).astype(np.int32).reshape(1, -1))
        target = lax.dynamic_index_in_dim(
            jnp.asarray(np.stack(targets)),
            lax.axis_index("gz") * gy + lax.axis_index("gy"),
            keepdims=False,
        )
        cot_sent = call(
            lambda *refs: unpack_cotangent_body(tz, *refs),
            "unpack_cotangent",
            flat,
            [vm((count, dim))],
            (target, packed(cotangent)),
            vmem_mib=10,
        ).reshape(gy, count // gy, dim)
        cot_own = [cot_sent[0]] + [
            lax.ppermute(cot_sent[k], "gy", [(i, i ^ k) for i in range(gy)])
            for k in range(1, gy)
        ]
        near = gy // 2
        parts = [
            jnp.concatenate([piece[piece.shape[0] // 2 :] for piece in pieces], 0)
            for pieces in (cot_own[:near], cot_own[near:])
        ]
        *parts, tok_x = lax.optimization_barrier((*parts, tok_x))
        cot_other = [lax.ppermute(part, "gz", [(0, 1), (1, 0)]) for part in parts]

        sent, qkv_x = call(
            lambda *refs: x_forward_body(line_shape, lines_x, *refs),
            "x_forward",
            (flat, jax.ShapeDtypeStruct((count, 3 * dim), BF16)),
            [
                vm((count, dim)),
                vm((count, dim)),
                vm((dim, 3 * dim)),
                vm((dim, dim)),
                pltpu.SemaphoreType.DMA((4,)),
            ],
            (gain_x, w_qkv_x, w_out_x, tok_x),
            vmem_mib=52,
            in_hbm=(1, 2),
            flops=3 * 10**9,
        )
        sent, cot_other[0] = lax.optimization_barrier((sent, cot_other[0]))
        s1_y = exchange(sent, ("gy", "gh"), gh * gy)

        def line_run(i, k):
            return slice((i * gy + k) * ty, (i * gy + k + 1) * ty)

        def grad_act(name, pieces, gather_rows):
            half = jax.ShapeDtypeStruct((count // 2, dim), BF16)
            return call(
                lambda *refs: grad_act_body(gather_rows, len(pieces), *refs),
                name,
                (half, jax.ShapeDtypeStruct((count // 2, hidden), BF16)),
                [],
                (*pieces, w_down),
                vmem_mib=16,
            )

        own_runs = [(line_run(i, k), k, i * ty) for i in range(own) for k in range(gy)]
        other_runs = [
            (line_run(i, k), k // near, (k % near * own + i) * ty)
            for i in range(own)
            for k in range(gy)
        ]
        cot_a, g_act_a = grad_act("grad_act_own", cot_own, own_runs)
        cot_b, g_act_b = grad_act("grad_act_other", cot_other, other_runs)

        g1_sent = call(
            lambda *refs: middle_body(lines_y, *refs),
            "middle",
            flat,
            [
                vm((count, dim)),
                vm((count, dim)),
                vm((count, dim)),
                vm((count, 3 * dim)),
                vm((count, dim)),
                vm((count, dim)),
                vm((x_lines * HEADS // GROUP, len_y, GROUP * len_y), F32),
                vm((count, dim), F32),
                vm((count, dim)),
                vm((count, 3 * dim)),
                vm((count, hidden)),
                vm((count, hidden)),
                vm((dim, 3 * dim)),
                vm((dim, dim)),
                vm((dim, hidden)),
                pltpu.SemaphoreType.DMA((4,)),
                pltpu.SemaphoreType.DMA((3,)),
            ],
            (
                s1_y, cot_a, cot_b, g_act_a, g_act_b, gain_y, gain_mlp,
                w_qkv_y, w_out_y, w_up,
            ),
            vmem_mib=52,
            in_hbm=(3, 4, 7, 8, 9),
            flops=9 * 10**9,
        )
        g1_x = exchange(g1_sent, ("gy", "gh"), gh * gy)

        gt_parts = call(
            lambda *refs: x_back_body(line_shape, lines_x, *refs),
            "x_back",
            [jax.ShapeDtypeStruct((count // gx, dim), BF16)] * gx,
            [
                vm((count, dim)),
                vm((count, dim)),
                vm((count, dim)),
                vm((count, dim)),
                vm((count, 3 * dim)),
                vm((count, dim), F32),
                vm((count, 3 * dim)),
                vm((dim, 3 * dim)),
                vm((dim, dim)),
                pltpu.SemaphoreType.DMA((2,)),
                pltpu.SemaphoreType.DMA((2,)),
            ],
            (g1_x, qkv_x, gain_x, w_qkv_x, w_out_x, tok_x),
            vmem_mib=52,
            in_hbm=(1, 3, 4, 5),
            flops=3 * 10**9,
        )
        gt = list(gt_parts)
        for k in [*range(gh, gx), *range(1, gh)]:
            gt[k] = lax.ppermute(gt[k], ("gz", "gh"), [(i, i ^ k) for i in range(gx)])
        out = call(
            lambda *refs: pack_body(tile, *refs),
            "pack",
            jax.ShapeDtypeStruct((count * tile.blocks, 128), BF16),
            [vm((count, dim))],
            tuple(gt),
            vmem_mib=10,
        )
        split = out.reshape(tx, ty, tile.blocks, tz, 128).transpose(0, 1, 3, 2, 4)
        return split.reshape(tx, ty, tz, dim)

    return local


def solution(mesh):
    gx, gy = mesh.shape["gx"], mesh.shape["gy"]
    halved = Mesh(mesh.devices.reshape(NZ, gx // NZ, gy), ("gz", "gh", "gy"))
    tile = P(("gz", "gh"), "gy", None, None)
    return jax.shard_map(
        make_local(gx // NZ, gy),
        mesh=halved,
        in_specs=(tile, tile) + (P(),) * 9,
        out_specs=tile,
        check_vma=False,
    )
```
